256 devices in a mesh: rows: 32 (over z, y), feat: 8 (over x, core).
Axes of the slice: x: 4, y: 4, z: 8, core: 2. Of those that a mesh axis runs over, the one named last changes fastest.
Arguments:
- tokens: bfloat16 [20480, 5120], P('rows', 'feat'), may hold values from -6 to 6
- cotangent: bfloat16 [20480, 2048], P('rows', 'feat'), may hold values from -1.5 to 1.5
- frozen_weight: bfloat16 [5120, 2048], P('feat', 'rows'), may hold values from -0.078125 to 0.078125
- adapter_down_weight: bfloat16 [128, 32, 5120], P('rows', None, 'feat'), may hold values from -0.078125 to 0.078125
- adapter_up_weight: bfloat16 [128, 32, 2048], P('rows', None, 'feat'), may hold values from -1 to 1
- sequence_first_rows: int32 [64], replicated, may hold values from 0 to 20479, as said below
- embodiment: int32 [64], replicated, may hold values from 0 to 127
- adapter_store_row: int32 [128], replicated, may hold values from 0 to 127, each once
Outputs:
- key_value_output: bfloat16 [20480, 2048], P('rows', 'feat')
- token_gradient: bfloat16 [20480, 5120], P('rows', 'feat')
- grad_down: float32 [128, 32, 5120], P('rows', None, 'feat')
- grad_up: float32 [128, 32, 2048], P('rows', None, 'feat')
The draws below stay inside these ranges and needn't reach their ends.
Inputs may be any that keep to these rules, and one draw needn't show every extreme that they name: sequence_first_rows[0] is 0, the values rise strictly, each block of 640 consecutive rows (rows b * 640 to (b + 1) * 640 - 1) holds exactly 2 of them, and the last one is 20479; sequence j holds the rows from sequence_first_rows[j] up to the next start.
All inputs are finite; a program needn't handle non-finite values.
Results may differ from the reference program's by a relative error of at most 0.023.
Values may be sent and summed in bfloat16 or wider, within the bound.
No kernel may reach another device: no remote copies, remote signals or barrier semaphores. Data moves between devices by JAX's collectives and lax.ppermute only.
A program may use at most 128 MiB of HBM per device.

```python
import math
import jax
import jax.numpy as jnp
import numpy as np
from jax import lax

MODEL_WIDTH = 5120
KEY_VALUE_WIDTH = 2048
ADAPTER_RANK = 32
ADAPTER_COUNT = 128
TOK_DEV = 640
SEQ_DEV = 2
TOKENS = 20480
SEQS = 64
N_ROWS = 32


def draw_sequence_first_rows(key, part):
    key = jax.random.fold_in(key, 11)
    blocks = TOKENS // TOK_DEV
    noise = jax.random.randint(key, (blocks, TOK_DEV), 0, 1 << 19).astype(jnp.int32)
    offset = jnp.arange(TOK_DEV, dtype=jnp.int32)[None, :]
    block_index = jnp.arange(blocks, dtype=jnp.int32)[:, None]
    scores = noise * TOK_DEV + offset
    forced = (block_index == 0) & (offset == 0) | (block_index == blocks - 1) & (offset == TOK_DEV - 1)
    scores = jnp.where(forced, -1, scores)
    picked = jnp.argsort(scores, axis=1, stable=True)[:, :SEQ_DEV].astype(jnp.int32)
    chosen = jnp.sort(picked, axis=1) + block_index * TOK_DEV
    return chosen.reshape(SEQS).astype(jnp.int32)


def plant(array, rng, smallest, high):
    spot = [jax.random.randint(jax.random.fold_in(rng, axis), (), 0, length) for axis, length in enumerate(array.shape)]
    main_axis = array.shape.index(max(array.shape))
    neighbour = spot[:main_axis] + [(spot[main_axis] + 1) % array.shape[main_axis]] + spot[main_axis + 1:]
    return array.at[tuple(spot)].set(smallest).at[tuple(neighbour)].set(high)


def level_of(key, dims, shards, smallest, top_value):
    def one(dim, blocks):
        draws = jax.random.uniform(jax.random.fold_in(jax.random.fold_in(key, 6), dim), (blocks,), jnp.float32, smallest / len(shards), top_value / len(shards))
        return jnp.repeat(jnp.exp(draws), dims[dim] // blocks).reshape((-1,) + (1,) * (len(dims) - dim - 1))

    loudness = one(*shards[0])
    for cut in shards[1:]:
        loudness = loudness * one(*cut)
    return loudness


def rank_bounds(count, lean):
    weights = [(1 << 20) // math.isqrt(standing ** lean) + 1 for standing in range(1, count + 1)]
    width = 1 + sum(weights) // (1 << 30)
    return np.cumsum(np.array([max(1, weight // width) for weight in weights]))


def skewed_ids(own_key, shape, count, slope):
    grid = rank_bounds(count, slope)
    lot = jax.random.randint(jax.random.fold_in(own_key, 1), shape, 0, int(grid[count - 1]))
    standing = jnp.searchsorted(jnp.asarray(grid, jnp.int32), lot, side="right")
    return jax.random.permutation(jax.random.fold_in(own_key, 2), count)[standing].astype(jnp.int32)


def centred(own_key, dims, width, most, shards=(), kind=jnp.bfloat16):
    drawn = width * jax.random.normal(own_key, dims, jnp.float32)
    if shards:
        drawn = drawn * level_of(own_key, dims, shards, -0.22, 0.18)
    return jnp.clip(drawn, -most, most).astype(kind)


def setup_inputs(seed: int = 0) -> dict:
    keys = jax.random.split(jax.random.key(seed), 9)
    return {
        "tokens": centred(keys[0], (TOKENS, MODEL_WIDTH), 1.0, 6.0, ((0, 32), (1, 8))),
        "cotangent": centred(keys[1], (TOKENS, KEY_VALUE_WIDTH), 0.25, 1.5, ((0, 32), (1, 8))),
        "frozen_weight": centred(keys[2], (MODEL_WIDTH, KEY_VALUE_WIDTH), MODEL_WIDTH ** -0.5, 0.078125, ((0, 8), (1, 32))),
        "adapter_down_weight": centred(keys[3], (ADAPTER_COUNT, ADAPTER_RANK, MODEL_WIDTH), MODEL_WIDTH ** -0.5, 0.078125, ((0, 32), (2, 8))),
        "adapter_up_weight": centred(keys[4], (ADAPTER_COUNT, ADAPTER_RANK, KEY_VALUE_WIDTH), ADAPTER_RANK ** -0.5, 1.0, ((0, 32), (2, 8))),
        "sequence_first_rows": draw_sequence_first_rows(jax.random.fold_in(keys[8], 71), 0),
        "embodiment": plant(skewed_ids(keys[6], (SEQS,), ADAPTER_COUNT, 2), jax.random.fold_in(keys[6], 3), 0, ADAPTER_COUNT - 1).astype(jnp.int32),
        "adapter_store_row": jax.random.permutation(keys[7], ADAPTER_COUNT).astype(jnp.int32),
    }


ADAPTER_SCALE = 0.5


def token_slots(sequence_first_rows, embodiment, adapter_store_row, offset_row, amount):
    position = offset_row + jnp.arange(amount, dtype=jnp.int32)
    segment_ids = jnp.sum((sequence_first_rows[None, :] <= position[:, None]).astype(jnp.int32), axis=1) - 1
    sequence_hit = segment_ids[:, None] == jnp.arange(sequence_first_rows.shape[0], dtype=jnp.int32)[None, :]
    token_embody = jnp.sum(jnp.where(sequence_hit, embodiment[None, :], 0), axis=1)
    adapter_hit = token_embody[:, None] == jnp.arange(adapter_store_row.shape[0], dtype=jnp.int32)[None, :]
    return jnp.sum(jnp.where(adapter_hit, adapter_store_row[None, :], 0), axis=1).astype(jnp.int32)


def reference(tokens, cotangent, frozen_weight, adapter_down_weight, adapter_up_weight, sequence_first_rows, embodiment, adapter_store_row):
    store_rows = token_slots(sequence_first_rows, embodiment, adapter_store_row, 0, TOKENS)
    token_blocks = tokens.reshape(N_ROWS, TOK_DEV, MODEL_WIDTH)
    cotangent_blocks = cotangent.reshape(N_ROWS, TOK_DEV, KEY_VALUE_WIDTH)
    row_blocks = store_rows.reshape(N_ROWS, TOK_DEV)

    def block_step(running, inputs):
        down_total, up_total = running
        block_tokens, block_cotangent, block_token_rows = inputs
        frozen_key_value = jnp.dot(block_tokens, frozen_weight, preferred_element_type=jnp.float32)
        down_store_rows = adapter_down_weight[block_token_rows].astype(jnp.float32)
        up_store_rows = adapter_up_weight[block_token_rows].astype(jnp.float32)
        widened_tokens = block_tokens.astype(jnp.float32)
        widened_cotangent = block_cotangent.astype(jnp.float32)
        low_narrow = jnp.einsum("td,trd->tr", widened_tokens, down_store_rows).astype(jnp.bfloat16)
        narrow_widened = lax.optimization_barrier(low_narrow).astype(jnp.float32)
        key_value_block = (frozen_key_value + ADAPTER_SCALE * jnp.einsum("qs,qsh->qh", narrow_widened, up_store_rows)).astype(jnp.bfloat16)
        back_narrow = jnp.einsum("tc,trc->tr", widened_cotangent, up_store_rows).astype(jnp.bfloat16)
        backward_wide = lax.optimization_barrier(back_narrow).astype(jnp.float32)
        frozen_backward = jnp.dot(block_cotangent, frozen_weight.T, preferred_element_type=jnp.float32)
        gradient_block = (frozen_backward + ADAPTER_SCALE * jnp.einsum("yc,yca->ya", backward_wide, down_store_rows)).astype(jnp.bfloat16)
        down_addend = jax.ops.segment_sum(ADAPTER_SCALE * backward_wide[:, :, None] * widened_tokens[:, None, :], block_token_rows, num_segments=ADAPTER_COUNT)
        up_addend = jax.ops.segment_sum(ADAPTER_SCALE * narrow_widened[:, :, None] * widened_cotangent[:, None, :], block_token_rows, num_segments=ADAPTER_COUNT)
        down_total = down_total + lax.optimization_barrier(down_addend.astype(jnp.bfloat16)).astype(jnp.float32)
        up_total = up_total + lax.optimization_barrier(up_addend.astype(jnp.bfloat16)).astype(jnp.float32)
        return (down_total, up_total), (key_value_block, gradient_block)

    start_totals = (jnp.zeros((ADAPTER_COUNT, ADAPTER_RANK, MODEL_WIDTH), jnp.float32), jnp.zeros((ADAPTER_COUNT, ADAPTER_RANK, KEY_VALUE_WIDTH), jnp.float32))
    totals, blocks = lax.scan(block_step, start_totals, (token_blocks, cotangent_blocks, row_blocks))
    return blocks[0].reshape(TOKENS, KEY_VALUE_WIDTH), blocks[1].reshape(TOKENS, MODEL_WIDTH), totals[0], totals[1]
```

```python
import jax
import jax.numpy as jnp
from jax import lax
from jax.experimental import pallas as pl
from jax.experimental.pallas import tpu as pltpu
from jax.sharding import Mesh
from jax.sharding import PartitionSpec as P

NZ, NY, NX, NC = 8, 4, 4, 2
RANK = 32
OWNED = 4
SLOTS = 3
SCALE = 0.5
VM = pl.BlockSpec(memory_space=pltpu.VMEM)
SM = pl.BlockSpec(memory_space=pltpu.SMEM)
BF = jnp.bfloat16
F32 = jnp.float32


def params(mib):
    return pltpu.CompilerParams(vmem_limit_bytes=mib * 1024 * 1024)


def cost(flops, moved):
    return pl.CostEstimate(flops=flops, bytes_accessed=moved, transcendentals=0)


def nt(a, b):
    return lax.dot_general(a, b, (((1,), (1,)), ((), ())), preferred_element_type=F32)


def nn(a, b):
    return lax.dot_general(a, b, (((1,), (0,)), ((), ())), preferred_element_type=F32)


def tn(a, b):
    return lax.dot_general(a, b, (((0,), (0,)), ((), ())), preferred_element_type=F32)


def slot_mask(cut_ref, k, amount):
    row = lax.broadcasted_iota(jnp.int32, (1, amount), 1)
    first, second = cut_ref[0], cut_ref[1]
    if k == 0:
        return row < first
    if k == 1:
        return (row >= first) & (row < second)
    return row >= second


def shift_matrix(yi, amount):
    i = lax.broadcasted_iota(jnp.int32, (amount, amount), 0)
    j = lax.broadcasted_iota(jnp.int32, (amount, amount), 1)
    at = j + yi * (amount // NY)
    at = jnp.where(at >= amount, at - amount, at)
    return (i == at).astype(F32).astype(BF)


def pick_kernel(at_ref, g_ref, *outs):
    for k in range(NY):
        for s in range(SLOTS):
            at = at_ref[k * SLOTS + s]
            here = at >= 0
            at = jnp.maximum(at, 0)
            zo, a = at // OWNED, at % OWNED
            down = g_ref[zo, pl.ds(pl.multiple_of(64 + a * RANK, RANK), RANK), :]
            up = g_ref[zo, pl.ds(pl.multiple_of(192 + (a % 2) * RANK, RANK), RANK), :]
            up = jnp.where(a >= 2, up[:, 256:512], up[:, 0:256])
            rows = slice(s * RANK, (s + 1) * RANK)
            outs[k][rows, 0:640] = jnp.where(here, down, jnp.zeros_like(down))
            outs[k][rows, 640:896] = jnp.where(here, up, jnp.zeros_like(up))


def low_kernel(cut_ref, a0, a1, a2, a3, tok_ref, cot_ref, part_ref, slots_ref):
    slots = (a0[...] + a1[...]) + (a2[...] + a3[...])
    slots_ref[...] = slots
    amount = tok_ref.shape[0]
    low = nt(slots[:, :640], tok_ref[...])
    back = nt(slots[:, 640:], cot_ref[...])
    low_sum = jnp.zeros((RANK, amount), F32)
    back_sum = jnp.zeros((RANK, amount), F32)
    for k in range(SLOTS):
        keep = slot_mask(cut_ref, k, amount)
        low_sum += jnp.where(keep, low[k * RANK:(k + 1) * RANK], 0.0)
        back_sum += jnp.where(keep, back[k * RANK:(k + 1) * RANK], 0.0)
    part_ref[0:RANK] = low_sum.astype(BF)
    part_ref[RANK:] = back_sum.astype(BF)


def term_kernel(cut_ref, p0, p1, p2, p3, tok_ref, cot_ref, term_ref, low_ref, back_ref):
    total = (p0[...].astype(F32) + p1[...].astype(F32)) + (p2[...].astype(F32) + p3[...].astype(F32))
    amount = tok_ref.shape[0]
    low, back = total[:RANK], total[RANK:]
    for k in range(SLOTS):
        keep = slot_mask(cut_ref, k, amount)
        low_ref[k * RANK:(k + 1) * RANK] = jnp.where(keep, low, 0.0).astype(BF)
        back_ref[k * RANK:(k + 1) * RANK] = jnp.where(keep, back, 0.0).astype(BF)
    term_ref[:, :640] = (SCALE * nn(back_ref[...], tok_ref[...])).astype(BF)
    term_ref[:, 640:] = (SCALE * nn(low_ref[...], cot_ref[...])).astype(BF)


def kv_send_kernel(xi_ref, w0, w1, w2, w3, tok_ref, out_ref):
    w = jnp.concatenate([w0[0], w1[0], w2[0], w3[0]], axis=0)
    out_ref[0] = nt(tok_ref[...], w).astype(BF)


def kv_keep_kernel(xi_ref, w0, w1, w2, w3, tok_ref, other_ref, out_ref):
    w = jnp.concatenate([w0[0], w1[0], w2[0], w3[0]], axis=0)
    out_ref[0] = (nt(tok_ref[...], w) + other_ref[0].astype(F32)).astype(BF)


def kv_out_kernel(yi_ref, p0, p1, p2, p3, low_ref, slots_ref, out_ref):
    shift = shift_matrix(yi_ref[0], out_ref.shape[1])
    up = nn(slots_ref[:, 640:], shift).astype(BF)
    total = (p0[...].astype(F32) + p1[...].astype(F32)) + (p2[...].astype(F32) + p3[...].astype(F32))
    total = (total + SCALE * tn(low_ref[...], up)).astype(BF)
    out_ref[...] = nt(total, shift).astype(BF)


def input_grad_kernel(w0, w1, w2, w3, cot_ref, back_ref, slots_ref, out_ref, acc_ref):
    f = pl.program_id(0)

    @pl.when(f == 0)
    def _():
        acc_ref[...] = SCALE * tn(back_ref[...], slots_ref[:, :640])

    w = jnp.concatenate([w0[0], w1[0], w2[0], w3[0]], axis=0)
    acc_ref[...] += nn(cot_ref[0], w)

    @pl.when(f == pl.num_programs(0) - 1)
    def _():
        out_ref[...] = acc_ref[...].astype(BF)


def bin_kernel(to_ref, t_ref, o0, o1, o2, o3, acc_ref):
    acc_ref[...] = jnp.zeros_like(acc_ref)
    for j in range(NZ * SLOTS):
        to = to_ref[j]

        @pl.when(to >= 0)
        def _(j=j, to=to):
            zs, s = j // SLOTS, j % SLOTS
            acc_ref[to] += t_ref[zs, s * RANK:(s + 1) * RANK, :].astype(F32)

    for k, o in enumerate((o0, o1, o2, o3)):
        for a in range(OWNED):
            o[a * RANK:(a + 1) * RANK] = acc_ref[k * OWNED + a].astype(BF)


def total_kernel(p0, p1, p2, p3, down_ref, up_ref):
    total = (p0[...].astype(F32) + p1[...].astype(F32)) + (p2[...].astype(F32) + p3[...].astype(F32))
    down_ref[...] = total[:, :640]
    up_ref[...] = total[:, 640:]


def ahead(value, axis, n, k):
    return lax.ppermute(value, axis, [(i, (i - k) % n) for i in range(n)])


def deliver(value, axis, n, k):
    return lax.ppermute(value, axis, [(i, (i + k) % n) for i in range(n)])


def on_device(tokens, cot, w, down, up, first_rows, embodiment, store_row):
    zi, yi = lax.axis_index("z"), lax.axis_index("y")
    xi, ci = lax.axis_index("x"), lax.axis_index("c")
    rows, dl = tokens.shape
    cl = cot.shape[1]
    block = zi * NY + yi
    width = dl + cl

    up2 = jnp.concatenate(
        [up[:2].reshape(2 * RANK, cl), up[2:].reshape(2 * RANK, cl), jnp.zeros((2 * RANK, dl - 2 * cl), BF)], axis=1
    )
    pack = jnp.concatenate([w.T, down.reshape(OWNED * RANK, dl), up2], axis=0)
    g = lax.all_gather(pack, "z")

    seq_count = first_rows.shape[0]
    emb_hit = embodiment[:, None] == jnp.arange(store_row.shape[0], dtype=jnp.int32)[None, :]
    seq_store = jnp.sum(jnp.where(emb_hit, store_row[None, :], 0), axis=1)

    def stores_of(blocks):
        seqs = (2 * blocks[:, None] - 1 + jnp.arange(SLOTS, dtype=jnp.int32)[None, :]).reshape(-1)
        hit = jnp.maximum(seqs, 0)[:, None] == jnp.arange(seq_count, dtype=jnp.int32)[None, :]
        return jnp.sum(jnp.where(hit, seq_store[None, :], 0), axis=1)

    ks = jnp.arange(NY, dtype=jnp.int32)
    plane = stores_of(zi * NY + (yi + ks) % NY)
    pick_at = jnp.where((plane // OWNED) % NY == yi, (plane // (OWNED * NY)) * OWNED + plane % OWNED, -1)
    line = stores_of(jnp.arange(NZ, dtype=jnp.int32) * NY + yi)
    bin_to = jnp.where(
        line // (OWNED * NY) == zi, (((line // OWNED) % NY - yi) % NY) * OWNED + line % OWNED, -1
    )
    cut = lax.dynamic_slice_in_dim(first_rows, 2 * block, 2) - block * rows
    yv = jnp.reshape(yi, (1,)).astype(jnp.int32)
    cv = jnp.stack([xi, ci]).astype(jnp.int32)

    picked = pl.pallas_call(
        pick_kernel,
        out_shape=[jax.ShapeDtypeStruct((SLOTS * RANK, width), BF)] * NY,
        in_specs=[SM, VM],
        out_specs=[VM] * NY,
        compiler_params=params(24),
        cost_estimate=cost(0, 3_000_000),
    )(pick_at, g)
    slot_parts = [picked[0]] + [deliver(picked[k], "y", NY, k) for k in range(1, NY)]

    w_own = g[:, :64]
    ws = [w_own] + [ahead(w_own, "y", NY, k) for k in range(1, NY)]

    i = jnp.arange(cl, dtype=jnp.int32)
    shift = (i[:, None] == ((i + yi * (cl // NY)) % cl)[None, :]).astype(BF)
    cot_moved = jnp.dot(cot, shift, preferred_element_type=F32).astype(BF)
    cot_moved, _ = lax.optimization_barrier((cot_moved, g))
    cot_all = lax.all_gather(cot_moved, ("x", "c"))

    part, slots = pl.pallas_call(
        low_kernel,
        out_shape=[
            jax.ShapeDtypeStruct((2 * RANK, rows), BF),
            jax.ShapeDtypeStruct((SLOTS * RANK, width), BF),
        ],
        in_specs=[SM] + [VM] * 6,
        out_specs=[VM, VM],
        compiler_params=params(24),
        cost_estimate=cost(2 * rows * SLOTS * RANK * width, 3_000_000),
    )(cut, *slot_parts, tokens, cot)
    part_other = lax.ppermute(part, "c", [(0, 1), (1, 0)])
    part = (part.astype(F32) + part_other.astype(F32)).astype(BF)
    parts = [part] + [ahead(part, "x", NX, k) for k in range(1, NX)]
    term, low, back = pl.pallas_call(
        term_kernel,
        out_shape=[
            jax.ShapeDtypeStruct((SLOTS * RANK, width), BF),
            jax.ShapeDtypeStruct((SLOTS * RANK, rows), BF),
            jax.ShapeDtypeStruct((SLOTS * RANK, rows), BF),
        ],
        in_specs=[SM] + [VM] * 6,
        out_specs=[VM] * 3,
        compiler_params=params(24),
        cost_estimate=cost(2 * rows * SLOTS * RANK * width, 3_000_000),
    )(cut, *parts, tokens, cot)
    terms = lax.all_gather(term, "z")

    def w_spec(own):
        def index(k, cv):
            return (2 * ((cv[0] + k) % NX) + (cv[1] if own else 1 - cv[1]), 0, 0)

        return pl.BlockSpec((1, 64, dl), index)

    whole = pl.BlockSpec((rows, dl), lambda k, cv: (0, 0))
    piece = pl.BlockSpec((1, rows, cl), lambda k, cv: (k, 0, 0))
    half = jax.ShapeDtypeStruct((NX, rows, cl), BF)
    kv_cost = cost(2 * rows * dl * cl * NX, 4_000_000)
    kv_send = pl.pallas_call(
        kv_send_kernel,
        grid_spec=pltpu.PrefetchScalarGridSpec(
            num_scalar_prefetch=1, grid=(NX,), in_specs=[w_spec(False)] * NY + [whole], out_specs=piece
        ),
        out_shape=half,
        compiler_params=params(24),
        cost_estimate=kv_cost,
    )(cv, *ws, tokens)
    kv_other = lax.ppermute(kv_send, "c", [(0, 1), (1, 0)])
    kv_keep = pl.pallas_call(
        kv_keep_kernel,
        grid_spec=pltpu.PrefetchScalarGridSpec(
            num_scalar_prefetch=1, grid=(NX,), in_specs=[w_spec(True)] * NY + [whole, piece], out_specs=piece
        ),
        out_shape=half,
        compiler_params=params(24),
        cost_estimate=kv_cost,
    )(cv, *ws, tokens, kv_other)
    kv_parts = [kv_keep[0]] + [deliver(kv_keep[k], "x", NX, k) for k in range(1, NX)]

    token_gradient = pl.pallas_call(
        input_grad_kernel,
        grid=(NZ,),
        in_specs=[pl.BlockSpec((1, 64, dl), lambda f: (f, 0, 0))] * NY
        + [
            pl.BlockSpec((1, rows, cl), lambda f: (f, 0, 0)),
            pl.BlockSpec((SLOTS * RANK, rows), lambda f: (0, 0)),
            pl.BlockSpec((SLOTS * RANK, width), lambda f: (0, 0)),
        ],
        out_specs=pl.BlockSpec((rows, dl), lambda f: (0, 0)),
        out_shape=jax.ShapeDtypeStruct((rows, dl), BF),
        scratch_shapes=[pltpu.VMEM((rows, dl), F32)],
        compiler_params=params(24),
        cost_estimate=cost(2 * rows * dl * cl * NZ, 7_000_000),
    )(*ws, cot_all, back, slots)

    key_value_output = pl.pallas_call(
        kv_out_kernel,
        out_shape=jax.ShapeDtypeStruct((rows, cl), BF),
        in_specs=[SM] + [VM] * 6,
        out_specs=VM,
        compiler_params=params(24),
        cost_estimate=cost(2 * rows * cl * 512, 2_000_000),
    )(yv, *kv_parts, low, slots)

    bins = pl.pallas_call(
        bin_kernel,
        out_shape=[jax.ShapeDtypeStruct((OWNED * RANK, width), BF)] * NY,
        in_specs=[SM, VM],
        out_specs=[VM] * NY,
        scratch_shapes=[pltpu.VMEM((NY * OWNED, RANK, width), F32)],
        compiler_params=params(24),
        cost_estimate=cost(0, 4_000_000),
    )(bin_to, terms)
    bin_parts = [bins[0]] + [deliver(bins[k], "y", NY, k) for k in range(1, NY)]
    grad_down, grad_up = pl.pallas_call(
        total_kernel,
        out_shape=[
            jax.ShapeDtypeStruct((OWNED * RANK, dl), F32),
            jax.ShapeDtypeStruct((OWNED * RANK, cl), F32),
        ],
        in_specs=[VM] * 4,
        out_specs=[VM, VM],
        compiler_params=params(24),
        cost_estimate=cost(0, 2_000_000),
    )(*bin_parts)
    return (
        key_value_output,
        token_gradient,
        grad_down.reshape(OWNED, RANK, dl),
        grad_up.reshape(OWNED, RANK, cl),
    )


def solution(mesh):
    fine = Mesh(mesh.devices.reshape(NZ, NY, NX, NC), ("z", "y", "x", "c"))
    rows, feat = ("z", "y"), ("x", "c")
    return jax.shard_map(
        on_device,
        mesh=fine,
        in_specs=(
            P(rows, feat),
            P(rows, feat),
            P(feat, rows),
            P(rows, None, feat),
            P(rows, None, feat),
            P(),
            P(),
            P(),
        ),
        out_specs=(
            P(rows, feat),
            P(rows, feat),
            P(rows, None, feat),
            P(rows, None, feat),
        ),
        check_vma=False,
    )
```

```python
import jax
import jax.numpy as jnp
from jax import lax
from jax.experimental import pallas as pl
from jax.experimental.pallas import tpu as pltpu
from jax.sharding import Mesh
from jax.sharding import PartitionSpec as P

NZ, NY, NX, NC = 8, 4, 4, 2
RANK = 32
OWNED = 4
SLOTS = 3
SCALE = 0.5
VM = pl.BlockSpec(memory_space=pltpu.VMEM)
SM = pl.BlockSpec(memory_space=pltpu.SMEM)
ANY = pl.BlockSpec(memory_space=pl.ANY)
BF = jnp.bfloat16
F32 = jnp.float32


def params(mib):
    return pltpu.CompilerParams(vmem_limit_bytes=mib * 1024 * 1024)


def cost(flops, moved):
    return pl.CostEstimate(flops=flops, bytes_accessed=moved, transcendentals=0)


def nt(a, b):
    return lax.dot_general(a, b, (((1,), (1,)), ((), ())), preferred_element_type=F32)


def nn(a, b):
    return lax.dot_general(a, b, (((1,), (0,)), ((), ())), preferred_element_type=F32)


def tn(a, b):
    return lax.dot_general(a, b, (((0,), (0,)), ((), ())), preferred_element_type=F32)


def slot_mask(cut_ref, k, amount):
    row = lax.broadcasted_iota(jnp.int32, (1, amount), 1)
    first, second = cut_ref[0], cut_ref[1]
    if k == 0:
        return row < first
    if k == 1:
        return (row >= first) & (row < second)
    return row >= second


def shift_matrix(yi, amount):
    i = lax.broadcasted_iota(jnp.int32, (amount, amount), 0)
    j = lax.broadcasted_iota(jnp.int32, (amount, amount), 1)
    at = j + yi * (amount // NY)
    at = jnp.where(at >= amount, at - amount, at)
    return (i == at).astype(F32).astype(BF)


def pack_kernel(yi_ref, wt_ref, down_ref, up_ref, cot_ref, out_ref, cot_out, cot_in, sems):
    copies = [
        pltpu.make_async_copy(source, target, sems.at[n])
        for n, (source, target) in enumerate(
            (
                (wt_ref, out_ref.at[0:64]),
                (down_ref, out_ref.at[64:192]),
                (up_ref.at[0:64], out_ref.at[192:256, 0:256]),
                (up_ref.at[64:128], out_ref.at[192:256, 256:512]),
                (cot_ref, cot_in),
            )
        )
    ]
    for copy in copies:
        copy.start()
    out_ref[192:256, 512:] = jnp.zeros((64, out_ref.shape[1] - 512), BF)
    shift = shift_matrix(yi_ref[0], cot_ref.shape[1])
    for copy in copies:
        copy.wait()
    cot_out[...] = nn(cot_in[...], shift).astype(BF)


def gather_pieces(all_ref, own, f, b):
    half = own.shape[0] // 2
    all_ref[0] = own[...]
    for k in range(1, NZ // 2):
        all_ref[NZ - k] = f[k - 1][...]
        all_ref[k] = b[k - 1][...]
    all_ref[NZ // 2, :half] = f[NZ // 2 - 1][...]
    all_ref[NZ // 2, half:] = b[NZ // 2 - 1][...]


def pick_kernel(at_ref, own, f1, f2, f3, f4, b1, b2, b3, b4, *rest):
    *cots, o0, o1, o2, o3, w_ref, cot_ref, g_ref = rest
    for k, cot in enumerate(cots):
        cot_ref[k] = cot[...]
    gather_pieces(g_ref, own, (f1, f2, f3, f4), (b1, b2, b3, b4))
    w_ref[...] = g_ref[:, :64, :]
    outs = (o0, o1, o2, o3)
    for k in range(NY):
        for s in range(SLOTS):
            at = at_ref[k * SLOTS + s]
            here = at >= 0
            at = jnp.maximum(at, 0)
            zo, a = at // OWNED, at % OWNED
            down = g_ref[zo, pl.ds(pl.multiple_of(64 + a * RANK, RANK), RANK), :]
            up = g_ref[zo, pl.ds(pl.multiple_of(192 + (a % 2) * RANK, RANK), RANK), :]
            up = jnp.where(a >= 2, up[:, 256:512], up[:, 0:256])
            rows = slice(s * RANK, (s + 1) * RANK)
            outs[k][rows, 0:640] = jnp.where(here, down, jnp.zeros_like(down))
            outs[k][rows, 640:896] = jnp.where(here, up, jnp.zeros_like(up))


def low_kernel(cut_ref, a0, a1, a2, a3, tok_ref, cot_ref, w_ref, _1, part_ref, slots_ref, w_out):
    w_out[...] = w_ref[...]
    slots = (a0[...] + a1[...]) + (a2[...] + a3[...])
    slots_ref[...] = slots
    amount = tok_ref.shape[0]
    low = nt(slots[:, :640], tok_ref[...])
    back = nt(slots[:, 640:], cot_ref[...])
    low_sum = jnp.zeros((RANK, amount), F32)
    back_sum = jnp.zeros((RANK, amount), F32)
    for k in range(SLOTS):
        keep = slot_mask(cut_ref, k, amount)
        low_sum += jnp.where(keep, low[k * RANK:(k + 1) * RANK], 0.0)
        back_sum += jnp.where(keep, back[k * RANK:(k + 1) * RANK], 0.0)
    part_ref[0:RANK] = low_sum.astype(BF)
    part_ref[RANK:] = back_sum.astype(BF)


def term_kernel(
    cut_ref, p0, p1, p2, p3, tok_ref, cot_ref, prev_ref, next_ref, term_ref, low_ref, back_ref, prev_half, next_half
):
    prev_half[...] = prev_ref[: NZ // 2]
    next_half[...] = next_ref[NZ // 2:]
    total = (p0[...].astype(F32) + p1[...].astype(F32)) + (p2[...].astype(F32) + p3[...].astype(F32))
    amount = tok_ref.shape[0]
    low, back = total[:RANK], total[RANK:]
    for k in range(SLOTS):
        keep = slot_mask(cut_ref, k, amount)
        low_ref[k * RANK:(k + 1) * RANK] = jnp.where(keep, low, 0.0).astype(BF)
        back_ref[k * RANK:(k + 1) * RANK] = jnp.where(keep, back, 0.0).astype(BF)
    term_ref[:, :640] = (SCALE * nn(back_ref[...], tok_ref[...])).astype(BF)
    term_ref[:, 640:] = (SCALE * nn(low_ref[...], cot_ref[...])).astype(BF)


def rows_of(ws, at):
    own, ahead_1, far_low, far_high, behind_1 = ws
    half = NZ // 2
    far = jnp.where(at < half, far_low[jnp.minimum(at, half - 1)], far_high[jnp.maximum(at - half, 0)])
    return jnp.concatenate([own[at], ahead_1[at], far, behind_1[at]], axis=0)


def kv_send_kernel(at_ref, w0, w1, w2, w3, w4, tok_ref, _1, _2, out_ref):
    def step(k, carry):
        out_ref[k] = nt(tok_ref[...], rows_of((w0, w1, w2, w3, w4), at_ref[NX + k])).astype(BF)
        return carry

    lax.fori_loop(0, NX, step, 0)


def kv_keep_kernel(at_ref, w0, w1, w2, w3, w4, tok_ref, other_ref, *outs):
    for k, out_ref in enumerate(outs):
        base = nt(tok_ref[...], rows_of((w0, w1, w2, w3, w4), at_ref[k]))
        out_ref[...] = (base + other_ref[k].astype(F32)).astype(BF)


def kv_out_kernel(yi_ref, p0, p1, p2, p3, low_ref, slots_ref, out_ref):
    shift = shift_matrix(yi_ref[0], out_ref.shape[1])
    up = nn(slots_ref[:, 640:], shift).astype(BF)
    total = (p0[...].astype(F32) + p1[...].astype(F32)) + (p2[...].astype(F32) + p3[...].astype(F32))
    total = (total + SCALE * tn(low_ref[...], up)).astype(BF)
    out_ref[...] = nt(total, shift).astype(BF)


def input_grad_kernel(at_ref, w0, w1, w2, w3, w4, own_ref, other_ref, back_ref, slots_ref, out_ref, acc_ref):
    ws = (w0, w1, w2, w3, w4)
    acc_ref[...] = SCALE * tn(back_ref[...], slots_ref[:, :640])

    def step(k, carry):
        acc_ref[...] += nn(own_ref[k], rows_of(ws, at_ref[k])) + nn(other_ref[k], rows_of(ws, at_ref[NX + k]))
        return carry

    lax.fori_loop(0, NX, step, 0)
    out_ref[...] = acc_ref[...].astype(BF)


def bin_kernel(to_ref, own, f1, f2, f3, f4, b1, b2, b3, b4, _1, o0, o1, o2, o3, t_ref, acc_ref):
    gather_pieces(t_ref, own, (f1, f2, f3, f4), (b1, b2, b3, b4))
    acc_ref[...] = jnp.zeros_like(acc_ref)
    for j in range(NZ * SLOTS):
        to = to_ref[j]

        @pl.when(to >= 0)
        def _(j=j, to=to):
            zs, s = j // SLOTS, j % SLOTS
            acc_ref[to] += t_ref[zs, s * RANK:(s + 1) * RANK, :].astype(F32)

    for k, o in enumerate((o0, o1, o2, o3)):
        for a in range(OWNED):
            o[a * RANK:(a + 1) * RANK] = acc_ref[k * OWNED + a].astype(BF)


def total_kernel(p0, p1, p2, p3, down_ref, up_ref):
    total = (p0[...].astype(F32) + p1[...].astype(F32)) + (p2[...].astype(F32) + p3[...].astype(F32))
    down_ref[...] = total[:, :640]
    up_ref[...] = total[:, 640:]


def ahead(value, axis, n, k):
    return lax.ppermute(value, axis, [(i, (i - k) % n) for i in range(n)])


def deliver(value, axis, n, k):
    return lax.ppermute(value, axis, [(i, (i + k) % n) for i in range(n)])


def ring(value):
    half = value.shape[0] // 2
    f, b = [value], [value]
    for _ in range(NZ // 2 - 1):
        f.append(deliver(f[-1], "z", NZ, 1))
        b.append(deliver(b[-1], "z", NZ, -1))
    f.append(deliver(f[-1][:half], "z", NZ, 1))
    b.append(deliver(b[-1][half:], "z", NZ, -1))
    return f[1:] + b[1:]


def on_device(tokens, cot, w, down, up, first_rows, embodiment, store_row):
    zi, yi = lax.axis_index("z"), lax.axis_index("y")
    xi, ci = lax.axis_index("x"), lax.axis_index("c")
    rows, dl = tokens.shape
    cl = cot.shape[1]
    block = zi * NY + yi
    width = dl + cl

    yv = jnp.reshape(yi, (1,)).astype(jnp.int32)
    pack, cot_moved = pl.pallas_call(
        pack_kernel,
        out_shape=[jax.ShapeDtypeStruct((256, dl), BF), jax.ShapeDtypeStruct((rows, cl), BF)],
        in_specs=[SM] + [ANY] * 4,
        out_specs=[VM] * 2,
        scratch_shapes=[pltpu.VMEM((rows, cl), BF), pltpu.SemaphoreType.DMA((5,))],
        compiler_params=params(4),
        cost_estimate=cost(0, 1_400_000),
    )(yv, w.T, down.reshape(OWNED * RANK, dl), up.reshape(OWNED * RANK, cl), cot)
    gathered = ring(pack)
    cot_x = [cot_moved] + [ahead(cot_moved, "x", NX, k) for k in range(1, NX)]

    seq_count = first_rows.shape[0]
    emb_hit = embodiment[:, None] == jnp.arange(store_row.shape[0], dtype=jnp.int32)[None, :]
    seq_store = jnp.sum(jnp.where(emb_hit, store_row[None, :], 0), axis=1)

    def stores_of(blocks):
        seqs = (2 * blocks[:, None] - 1 + jnp.arange(SLOTS, dtype=jnp.int32)[None, :]).reshape(-1)
        hit = jnp.maximum(seqs, 0)[:, None] == jnp.arange(seq_count, dtype=jnp.int32)[None, :]
        return jnp.sum(jnp.where(hit, seq_store[None, :], 0), axis=1)

    ks = jnp.arange(NY, dtype=jnp.int32)
    plane = stores_of(zi * NY + (yi + ks) % NY)
    pick_at = jnp.where(
        (plane // OWNED) % NY == yi, ((plane // (OWNED * NY) - zi) % NZ) * OWNED + plane % OWNED, -1
    )
    line = stores_of(((zi + jnp.arange(NZ, dtype=jnp.int32)) % NZ) * NY + yi)
    bin_to = jnp.where(
        line // (OWNED * NY) == zi, (((line // OWNED) % NY - yi) % NY) * OWNED + line % OWNED, -1
    )
    cut = lax.dynamic_slice_in_dim(first_rows, 2 * block, 2) - block * rows
    home = 2 * ((xi + jnp.arange(NX, dtype=jnp.int32)) % NX)
    w_at = jnp.concatenate([home + ci, home + 1 - ci])
    w_at = ((w_at - zi) % NZ).astype(jnp.int32)

    *picked, w_own, cot_own = pl.pallas_call(
        pick_kernel,
        out_shape=[jax.ShapeDtypeStruct((SLOTS * RANK, width), BF)] * NY
        + [jax.ShapeDtypeStruct((NZ, 64, dl), BF), jax.ShapeDtypeStruct((NX, rows, cl), BF)],
        in_specs=[SM] + [VM] * 13,
        out_specs=[VM] * (NY + 2),
        scratch_shapes=[pltpu.VMEM((NZ, 256, dl), BF)],
        compiler_params=params(12),
        cost_estimate=cost(0, 9_000_000),
    )(pick_at, pack, *gathered, *cot_x)
    slot_parts = [picked[0]] + [deliver(picked[k], "y", NY, k) for k in range(1, NY)]

    cot_other = lax.ppermute(cot_own, "c", [(0, 1), (1, 0)])

    part, slots, w_own = pl.pallas_call(
        low_kernel,
        out_shape=[
            jax.ShapeDtypeStruct((2 * RANK, rows), BF),
            jax.ShapeDtypeStruct((SLOTS * RANK, width), BF),
            jax.ShapeDtypeStruct((NZ, 64, dl), BF),
        ],
        in_specs=[SM] + [VM] * 8,
        out_specs=[VM] * 3,
        compiler_params=params(12),
        cost_estimate=cost(2 * rows * SLOTS * RANK * width, 3_000_000),
    )(cut, *slot_parts, tokens, cot, w_own, cot_other)

    w_prev, w_next = deliver(w_own, "y", NY, 1), deliver(w_own, "y", NY, -1)

    part_other = lax.ppermute(part, "c", [(0, 1), (1, 0)])
    part = (part.astype(F32) + part_other.astype(F32)).astype(BF)
    parts = [part] + [ahead(part, "x", NX, k) for k in range(1, NX)]
    term, low, back, prev_half, next_half = pl.pallas_call(
        term_kernel,
        out_shape=[
            jax.ShapeDtypeStruct((SLOTS * RANK, width), BF),
            jax.ShapeDtypeStruct((SLOTS * RANK, rows), BF),
            jax.ShapeDtypeStruct((SLOTS * RANK, rows), BF),
            jax.ShapeDtypeStruct((NZ // 2, 64, dl), BF),
            jax.ShapeDtypeStruct((NZ // 2, 64, dl), BF),
        ],
        in_specs=[SM] + [VM] * 8,
        out_specs=[VM] * 5,
        compiler_params=params(12),
        cost_estimate=cost(2 * rows * SLOTS * RANK * width, 3_000_000),
    )(cut, *parts, tokens, cot, w_prev, w_next)
    terms = ring(term)
    w_far = [deliver(prev_half, "y", NY, 1), deliver(next_half, "y", NY, -1)]
    ws = [w_own, w_next, *w_far, w_prev]

    half = jax.ShapeDtypeStruct((NX, rows, cl), BF)
    kv_cost = cost(2 * rows * dl * cl * NX, 4_000_000)
    kv_send = pl.pallas_call(
        kv_send_kernel,
        out_shape=half,
        in_specs=[SM] + [VM] * 8,
        out_specs=VM,
        compiler_params=params(12),
        cost_estimate=kv_cost,
    )(w_at, *ws, tokens, terms[1], terms[NZ // 2 + 1])
    kv_other = lax.ppermute(kv_send, "c", [(0, 1), (1, 0)])
    kv_keep = pl.pallas_call(
        kv_keep_kernel,
        out_shape=[jax.ShapeDtypeStruct((rows, cl), BF)] * NX,
        in_specs=[SM] + [VM] * 7,
        out_specs=[VM] * NX,
        compiler_params=params(12),
        cost_estimate=kv_cost,
    )(w_at, *ws, tokens, kv_other)
    kv_parts = [kv_keep[0]] + [deliver(kv_keep[k], "x", NX, k) for k in range(1, NX)]

    token_gradient = pl.pallas_call(
        input_grad_kernel,
        out_shape=jax.ShapeDtypeStruct((rows, dl), BF),
        in_specs=[SM] + [VM] * 9,
        out_specs=VM,
        scratch_shapes=[pltpu.VMEM((rows, dl), F32)],
        compiler_params=params(12),
        cost_estimate=cost(20 * rows * dl * cl * NZ, 7_000_000),
    )(w_at, *ws, cot_own, cot_other, back, slots)

    key_value_output = pl.pallas_call(
        kv_out_kernel,
        out_shape=jax.ShapeDtypeStruct((rows, cl), BF),
        in_specs=[SM] + [VM] * 6,
        out_specs=VM,
        compiler_params=params(12),
        cost_estimate=cost(2 * rows * cl * 512, 2_000_000),
    )(yv, *kv_parts, low, slots)

    bins = pl.pallas_call(
        bin_kernel,
        out_shape=[jax.ShapeDtypeStruct((OWNED * RANK, width), BF)] * NY,
        in_specs=[SM] + [VM] * 10,
        out_specs=[VM] * NY,
        scratch_shapes=[pltpu.VMEM((NZ, SLOTS * RANK, width), BF), pltpu.VMEM((NY * OWNED, RANK, width), F32)],
        compiler_params=params(12),
        cost_estimate=cost(0, 4_000_000),
    )(bin_to, term, *terms, kv_keep[0])
    bin_parts = [bins[0]] + [deliver(bins[k], "y", NY, k) for k in range(1, NY)]
    grad_down, grad_up = pl.pallas_call(
        total_kernel,
        out_shape=[
            jax.ShapeDtypeStruct((OWNED * RANK, dl), F32),
            jax.ShapeDtypeStruct((OWNED * RANK, cl), F32),
        ],
        in_specs=[VM] * 4,
        out_specs=[VM, VM],
        compiler_params=params(12),
        cost_estimate=cost(0, 2_000_000),
    )(*bin_parts)
    return (
        key_value_output,
        token_gradient,
        grad_down.reshape(OWNED, RANK, dl),
        grad_up.reshape(OWNED, RANK, cl),
    )


def solution(mesh):
    fine = Mesh(mesh.devices.reshape(NZ, NY, NX, NC), ("z", "y", "x", "c"))
    rows, feat = ("z", "y"), ("x", "c")
    return jax.shard_map(
        on_device,
        mesh=fine,
        in_specs=(
            P(rows, feat),
            P(rows, feat),
            P(feat, rows),
            P(rows, None, feat),
            P(rows, None, feat),
            P(),
            P(),
            P(),
        ),
        out_specs=(
            P(rows, feat),
            P(rows, feat),
            P(rows, None, feat),
            P(rows, None, feat),
        ),
        check_vma=False,
    )
```

```python
import jax
import jax.numpy as jnp
from jax import lax
from jax.experimental import pallas as pl
from jax.experimental.pallas import tpu as pltpu
from jax.sharding import Mesh
from jax.sharding import PartitionSpec as P

NZ, NY, NX, NC = 8, 4, 4, 2
RANK = 32
OWNED = 4
SLOTS = 3
SCALE = 0.5
VM = pl.BlockSpec(memory_space=pltpu.VMEM)
SM = pl.BlockSpec(memory_space=pltpu.SMEM)
ANY = pl.BlockSpec(memory_space=pl.ANY)
HB = pl.BlockSpec(memory_space=pltpu.HBM)
BF = jnp.bfloat16
F32 = jnp.float32


def near(value):
    return pltpu.with_memory_space_constraint(value, pltpu.VMEM)


def far(value):
    return pltpu.with_memory_space_constraint(value, pltpu.HBM)


def made(*shape):
    return pltpu.VMEM(shape, BF)


def made_far(*shape):
    return pltpu.HBM(shape, BF)


def copy_all(pairs, sems):
    copies = [pltpu.make_async_copy(source, target, sems.at[n]) for n, (source, target) in enumerate(pairs)]
    for copy in copies:
        copy.start()
    for copy in copies:
        copy.wait()


def params(mib):
    return pltpu.CompilerParams(vmem_limit_bytes=mib * 1024 * 1024)


def cost(flops, moved):
    return pl.CostEstimate(flops=flops, bytes_accessed=moved, transcendentals=0)


def nt(a, b):
    return lax.dot_general(a, b, (((1,), (1,)), ((), ())), preferred_element_type=F32)


def nn(a, b):
    return lax.dot_general(a, b, (((1,), (0,)), ((), ())), preferred_element_type=F32)


def tn(a, b):
    return lax.dot_general(a, b, (((0,), (0,)), ((), ())), preferred_element_type=F32)


def slot_mask(cut_ref, k, amount):
    row = lax.broadcasted_iota(jnp.int32, (1, amount), 1)
    first, second = cut_ref[0], cut_ref[1]
    if k == 0:
        return row < first
    if k == 1:
        return (row >= first) & (row < second)
    return row >= second


def shift_matrix(yi, amount):
    i = lax.broadcasted_iota(jnp.int32, (amount, amount), 0)
    j = lax.broadcasted_iota(jnp.int32, (amount, amount), 1)
    at = j + yi * (amount // NY)
    at = jnp.where(at >= amount, at - amount, at)
    return (i == at).astype(F32).astype(BF)


def pack_kernel(wt_ref, down_ref, up_ref, out_ref, sems):
    copy_all(
        (
            (wt_ref, out_ref.at[0:64]),
            (down_ref, out_ref.at[64:192]),
            (up_ref.at[0:64], out_ref.at[192:256, 0:256]),
            (up_ref.at[64:128], out_ref.at[192:256, 256:512]),
            (up_ref.at[0:64, 0:128], out_ref.at[192:256, 512:640]),
        ),
        sems,
    )


def turn_kernel(yi_ref, _1, cot_ref, out_ref):
    out_ref[...] = nn(cot_ref[...], shift_matrix(yi_ref[0], cot_ref.shape[1])).astype(BF)


def gather_pieces(all_ref, own, f, b, first):
    for k, piece in enumerate((own, *b, *f[::-1])):
        all_ref[k] = piece[first:]


def pick_kernel(at_ref, own, f1, f2, f3, f4, b1, b2, b3, *refs):
    o0, o1, o2, o3, w_ref, *_, g_ref = refs[NX:]
    gather_pieces(g_ref, own, (f1, f2, f3, f4), (b1, b2, b3), 64)
    for k, piece in enumerate((own, b1, b2, b3, f4, f3, f2, f1)):
        w_ref[k] = piece[:64]
    outs = (o0, o1, o2, o3)
    for k in range(NY):
        for s in range(SLOTS):
            at = at_ref[k * SLOTS + s]
            here = at >= 0
            at = jnp.maximum(at, 0)
            zo, a = at // OWNED, at % OWNED
            down = g_ref[zo, pl.ds(pl.multiple_of(a * RANK, RANK), RANK), :]
            up = g_ref[zo, pl.ds(pl.multiple_of(128 + (a % 2) * RANK, RANK), RANK), :]
            up = jnp.where(a >= 2, up[:, 256:512], up[:, 0:256])
            rows = slice(s * RANK, (s + 1) * RANK)
            outs[k][rows, 0:640] = jnp.where(here, down, jnp.zeros_like(down))
            outs[k][rows, 640:896] = jnp.where(here, up, jnp.zeros_like(up))


def low_kernel(cut_ref, a0, a1, a2, a3, tok_ref, cot_ref, *refs):
    part_ref, slots_ref = refs[-3:-1]
    slots = (a0[...] + a1[...]) + (a2[...] + a3[...])
    slots_ref[...] = slots
    amount = tok_ref.shape[0]
    low = nt(slots[:, :640], tok_ref[...])
    back = nt(slots[:, 640:], cot_ref[...])
    low_sum = jnp.zeros((RANK, amount), F32)
    back_sum = jnp.zeros((RANK, amount), F32)
    for k in range(SLOTS):
        keep = slot_mask(cut_ref, k, amount)
        low_sum += jnp.where(keep, low[k * RANK:(k + 1) * RANK], 0.0)
        back_sum += jnp.where(keep, back[k * RANK:(k + 1) * RANK], 0.0)
    part_ref[0:RANK] = low_sum.astype(BF)
    part_ref[RANK:] = back_sum.astype(BF)


def term_kernel(cut_ref, p0, p1, p2, p3, tok_ref, cot_ref, term_ref, low_ref, back_ref):
    total = (p0[...].astype(F32) + p1[...].astype(F32)) + (p2[...].astype(F32) + p3[...].astype(F32))
    amount = tok_ref.shape[0]
    low, back = total[:RANK], total[RANK:]
    for k in range(SLOTS):
        keep = slot_mask(cut_ref, k, amount)
        low_ref[k * RANK:(k + 1) * RANK] = jnp.where(keep, low, 0.0).astype(BF)
        back_ref[k * RANK:(k + 1) * RANK] = jnp.where(keep, back, 0.0).astype(BF)
    term_ref[:, :640] = (SCALE * nn(back_ref[...], tok_ref[...])).astype(BF)
    term_ref[:, 640:] = (SCALE * nn(low_ref[...], cot_ref[...])).astype(BF)


def forward_kernel(_1, prev_ref, next_ref, c0, c1, c2, c3, prev_half, next_half, *refs):
    *_, buf_ref, sems = refs
    half = NZ // 2
    copy_all(((prev_ref.at[:half], buf_ref.at[0]), (next_ref.at[half:], buf_ref.at[1])), sems)
    copy_all(((buf_ref.at[0], prev_half), (buf_ref.at[1], next_half)), sems)


def load_weight(refs, w_ref, sems):
    half = NZ // 2
    own, ahead_1, far_low, far_high, behind_1 = refs
    copies = []
    for n, (ref, z, y) in enumerate(
        ((own, slice(0, NZ), 0), (ahead_1, slice(0, NZ), 1), (far_low, slice(0, half), 2), (far_high, slice(half, NZ), 2), (behind_1, slice(0, NZ), 3))
    ):
        copies.append(pltpu.make_async_copy(ref, w_ref.at[z, y * 64:(y + 1) * 64], sems.at[n]))
    for copy in copies:
        copy.start()
    return copies


def load_slices(refs, at_ref, first, w_ref, sems, start):
    half = NZ // 2
    own, ahead_1, far_low, far_high, behind_1 = refs

    def move(ref, z, k, y):
        copy = pltpu.make_async_copy(ref.at[z], w_ref.at[k, y * 64:(y + 1) * 64], sems.at[k, y])
        if start:
            copy.start()
        else:
            copy.wait()

    for k in range(NX):
        at = at_ref[first + k]
        for y, ref in ((0, own), (1, ahead_1), (3, behind_1)):
            move(ref, at, k, y)

        @pl.when(at < half)
        def _(k=k, at=at):
            move(far_low, at, k, 2)

        @pl.when(at >= half)
        def _(k=k, at=at):
            move(far_high, at - half, k, 2)


def wait_all(copies):
    for copy in copies:
        copy.wait()


def kv_send_kernel(at_ref, *refs):
    tok_ref, _, _, out_ref, w_ref, sems = refs[5:]
    load_slices(refs[:5], at_ref, NX, w_ref, sems, True)
    load_slices(refs[:5], at_ref, NX, w_ref, sems, False)

    def step(k, carry):
        out_ref[k] = nt(tok_ref[...], w_ref[k]).astype(BF)
        return carry

    lax.fori_loop(0, NX, step, 0)


def kv_keep_kernel(at_ref, *refs):
    tok_ref, other_ref, *outs, w_ref, sems = refs[5:]
    load_slices(refs[:5], at_ref, 0, w_ref, sems, True)
    load_slices(refs[:5], at_ref, 0, w_ref, sems, False)
    for k, out_ref in enumerate(outs):
        base = nt(tok_ref[...], w_ref[k])
        out_ref[...] = (base + other_ref[k].astype(F32)).astype(BF)


def kv_out_kernel(yi_ref, p0, p1, p2, p3, low_ref, slots_ref, out_ref):
    shift = shift_matrix(yi_ref[0], out_ref.shape[1])
    up = nn(slots_ref[:, 640:], shift).astype(BF)
    total = (p0[...].astype(F32) + p1[...].astype(F32)) + (p2[...].astype(F32) + p3[...].astype(F32))
    total = (total + SCALE * tn(low_ref[...], up)).astype(BF)
    out_ref[...] = nt(total, shift).astype(BF)


def input_grad_kernel(at_ref, *refs):
    cots = refs[5:5 + 2 * NX]
    back_ref, slots_ref, out_ref, acc_ref, w_ref, sems = refs[5 + 2 * NX:]
    copies = load_weight(refs[:5], w_ref, sems)
    acc_ref[...] = SCALE * tn(back_ref[...], slots_ref[:, :640])
    wait_all(copies)
    for k in range(NX):
        acc_ref[...] += nn(cots[k][...], w_ref[at_ref[k]]) + nn(cots[NX + k][...], w_ref[at_ref[NX + k]])
    out_ref[...] = acc_ref[...].astype(BF)


def bin_kernel(to_ref, own, f1, f2, f3, f4, b1, b2, b3, _1, out_ref, t_ref, acc_ref):
    gather_pieces(t_ref, own, (f1, f2, f3, f4), (b1, b2, b3), 0)
    acc_ref[...] = jnp.zeros_like(acc_ref)
    for j in range(NZ * SLOTS):
        to = to_ref[j]

        @pl.when(to >= 0)
        def _(j=j, to=to):
            zs, s = j // SLOTS, j % SLOTS
            acc_ref[to] += t_ref[zs, s * RANK:(s + 1) * RANK, :].astype(F32)

    for k in range(NY):
        for a in range(OWNED):
            out_ref[k, a * RANK:(a + 1) * RANK] = acc_ref[k * OWNED + a].astype(BF)


def total_kernel(in_ref, down_ref, up_ref):
    p0, p1, p2, p3 = (in_ref[k].astype(F32) for k in range(NY))
    total = (p0 + p1) + (p2 + p3)
    down_ref[...] = total[:, :640]
    up_ref[...] = total[:, 640:]


def others(axis, n, move, values):
    return [values[0]] + [move(values[k], axis, n, k) for k in range(1, n)]


def ahead(value, axis, n, k):
    return lax.ppermute(value, axis, [(i, (i - k) % n) for i in range(n)])


def deliver(value, axis, n, k):
    return lax.ppermute(value, axis, [(i, (i + k) % n) for i in range(n)])


def ring(value):
    f, b = [value], [value]
    for _ in range(NZ // 2 - 1):
        f.append(deliver(f[-1], "z", NZ, 1))
        b.append(deliver(b[-1], "z", NZ, -1))
    f.append(deliver(f[-1], "z", NZ, 1))
    return f[1:] + b[1:]


def on_device(tokens, cot, w, down, up, first_rows, embodiment, store_row):
    zi, yi = lax.axis_index("z"), lax.axis_index("y")
    xi, ci = lax.axis_index("x"), lax.axis_index("c")
    rows, dl = tokens.shape
    cl = cot.shape[1]
    block = zi * NY + yi
    width = dl + cl

    yv = jnp.reshape(yi, (1,)).astype(jnp.int32)
    pack = pl.pallas_call(
        pack_kernel,
        out_shape=made(256, dl),
        in_specs=[HB] * 3,
        out_specs=VM,
        scratch_shapes=[pltpu.SemaphoreType.DMA((5,))],
        compiler_params=params(4),
        cost_estimate=cost(0, 700_000),
    )(far(w.T), far(down.reshape(OWNED * RANK, dl)), far(up.reshape(OWNED * RANK, cl)))
    cot_moved = pl.pallas_call(
        turn_kernel,
        out_shape=made_far(rows, cl),
        in_specs=[SM, ANY, VM],
        out_specs=VM,
        compiler_params=params(4),
        cost_estimate=cost(0, 700_000),
    )(yv, pack, far(cot))
    gathered = ring(pack)
    cot_x = others("x", NX, ahead, [cot_moved] * NX)

    seq_count = first_rows.shape[0]
    emb_hit = embodiment[:, None] == jnp.arange(store_row.shape[0], dtype=jnp.int32)[None, :]
    seq_store = jnp.sum(jnp.where(emb_hit, store_row[None, :], 0), axis=1)

    def stores_of(blocks):
        seqs = (2 * blocks[:, None] - 1 + jnp.arange(SLOTS, dtype=jnp.int32)[None, :]).reshape(-1)
        hit = jnp.maximum(seqs, 0)[:, None] == jnp.arange(seq_count, dtype=jnp.int32)[None, :]
        return jnp.sum(jnp.where(hit, seq_store[None, :], 0), axis=1)

    ks = jnp.arange(NY, dtype=jnp.int32)
    plane = stores_of(zi * NY + (yi + ks) % NY)
    pick_at = jnp.where(
        (plane // OWNED) % NY == yi, ((plane // (OWNED * NY) - zi) % NZ) * OWNED + plane % OWNED, -1
    )
    line = stores_of(((zi + jnp.arange(NZ, dtype=jnp.int32)) % NZ) * NY + yi)
    bin_to = jnp.where(
        line // (OWNED * NY) == zi, line % (OWNED * NY), -1
    )
    cut = lax.dynamic_slice_in_dim(first_rows, 2 * block, 2) - block * rows
    home = 2 * ((xi + jnp.arange(NX, dtype=jnp.int32)) % NX)
    w_at = jnp.concatenate([home + ci, home + 1 - ci])
    w_at = ((w_at - zi) % NZ).astype(jnp.int32)

    picked = pl.pallas_call(
        pick_kernel,
        out_shape=[made(SLOTS * RANK, width)] * NY
        + [made_far(NZ, 64, dl)]
        + [made_far(rows, cl)] * NX,
        in_specs=[SM] + [VM] * 8 + [ANY] * NX,
        out_specs=[VM] * (NY + 1) + [ANY] * NX,
        input_output_aliases={9 + k: NY + 1 + k for k in range(NX)},
        scratch_shapes=[pltpu.VMEM((NZ, 192, dl), BF)],
        compiler_params=params(6),
        cost_estimate=cost(0, 9_000_000),
    )(pick_at, *map(near, (pack, *gathered)), *map(far, cot_x))
    w_own, cot_x = picked[NY], picked[NY + 1:]
    slot_parts = others("y", NY, deliver, picked)


    part, slots, w_own = pl.pallas_call(
        low_kernel,
        out_shape=[
            made(2 * RANK, rows),
            made(SLOTS * RANK, width),
            made_far(NZ, 64, dl),
        ],
        in_specs=[SM] + [VM] * 6 + [ANY],
        out_specs=[VM, VM, ANY],
        input_output_aliases={7: 2},
        compiler_params=params(6),
        cost_estimate=cost(2 * rows * SLOTS * RANK * width, 3_000_000),
    )(cut, *map(near, slot_parts), tokens, cot, far(w_own))

    w_prev, w_next = deliver(w_own, "y", NY, 1), deliver(w_own, "y", NY, -1)

    part_other = lax.ppermute(part, "c", [(0, 1), (1, 0)])
    part = (part.astype(F32) + part_other.astype(F32)).astype(BF)
    parts = others("x", NX, ahead, [part] * NX)
    term, low, back = pl.pallas_call(
        term_kernel,
        out_shape=[
            made(SLOTS * RANK, width),
            made(SLOTS * RANK, rows),
            made(SLOTS * RANK, rows),
        ],
        in_specs=[SM] + [VM] * 6,
        out_specs=[VM] * 3,
        compiler_params=params(6),
        cost_estimate=cost(2 * rows * SLOTS * RANK * width, 3_000_000),
    )(cut, *map(near, parts), tokens, cot)
    terms = ring(term)
    prev_half, next_half, *cot_x = pl.pallas_call(
        forward_kernel,
        out_shape=[made_far(NZ // 2, 64, dl)] * 2 + [made_far(rows, cl)] * NX,
        in_specs=[ANY, HB, HB] + [ANY] * NX,
        out_specs=[HB, HB] + [ANY] * NX,
        input_output_aliases={3 + k: 2 + k for k in range(NX)},
        scratch_shapes=[pltpu.VMEM((2, NZ // 2, 64, dl), BF), pltpu.SemaphoreType.DMA((2,))],
        compiler_params=params(4),
        cost_estimate=cost(0, 1_000),
    )(term, far(w_prev), far(w_next), *map(far, cot_x))
    far_low, far_high = deliver(prev_half, "y", NY, 1), deliver(next_half, "y", NY, -1)
    ws = [far(v) for v in (w_own, w_next, far_low, far_high, w_prev)]
    cot_other = [lax.ppermute(c, "c", [(0, 1), (1, 0)]) for c in cot_x]

    half = made_far(NX, rows, cl)
    kv_cost = cost(1_000, 1_000)
    kv_send = pl.pallas_call(
        kv_send_kernel,
        out_shape=half,
        in_specs=[SM] + [HB] * 5 + [VM] * 3,
        out_specs=VM,
        scratch_shapes=[pltpu.VMEM((NX, cl, dl), BF), pltpu.SemaphoreType.DMA((NX, NY))],
        compiler_params=params(16),
        cost_estimate=kv_cost,
    )(w_at, *ws, tokens, near(terms[2]), near(terms[NZ // 2 + 2]))
    kv_other = lax.ppermute(kv_send, "c", [(0, 1), (1, 0)])
    kv_keep = pl.pallas_call(
        kv_keep_kernel,
        out_shape=[made_far(rows, cl)] * NX,
        in_specs=[SM] + [HB] * 5 + [VM] * 2,
        out_specs=[VM] * NX,
        scratch_shapes=[pltpu.VMEM((NX, cl, dl), BF), pltpu.SemaphoreType.DMA((NX, NY))],
        compiler_params=params(16),
        cost_estimate=kv_cost,
    )(w_at, *ws, tokens, far(kv_other))
    kv_parts = others("x", NX, deliver, kv_keep)

    token_gradient = pl.pallas_call(
        input_grad_kernel,
        out_shape=jax.ShapeDtypeStruct((rows, dl), BF),
        in_specs=[SM] + [HB] * 5 + [VM] * (2 * NX + 2),
        out_specs=VM,
        scratch_shapes=[
            pltpu.VMEM((rows, dl), F32),
            pltpu.VMEM((NZ, cl, dl), BF),
            pltpu.SemaphoreType.DMA((5,)),
        ],
        compiler_params=params(16),
        cost_estimate=cost(20 * rows * dl * cl * NZ, 7_000_000),
    )(w_at, *ws, *map(far, (*cot_x, *cot_other)), near(back), near(slots))

    key_value_output = pl.pallas_call(
        kv_out_kernel,
        out_shape=jax.ShapeDtypeStruct((rows, cl), BF),
        in_specs=[SM] + [VM] * 6,
        out_specs=VM,
        compiler_params=params(8),
        cost_estimate=cost(2 * rows * cl * 512, 2_000_000),
    )(yv, *map(far, kv_parts), near(low), near(slots))

    bins = pl.pallas_call(
        bin_kernel,
        out_shape=made(NY, OWNED * RANK, width),
        in_specs=[SM] + [VM] * 8 + [ANY],
        out_specs=VM,
        scratch_shapes=[pltpu.VMEM((NZ, SLOTS * RANK, width), BF), pltpu.VMEM((NY * OWNED, RANK, width), F32)],
        compiler_params=params(8),
        cost_estimate=cost(0, 4_000_000),
    )(bin_to, *map(near, (term, *terms)), far(kv_keep[0]))
    bin_parts = lax.all_to_all(bins, "y", 0, 0, tiled=True)
    grad_down, grad_up = pl.pallas_call(
        total_kernel,
        out_shape=[
            jax.ShapeDtypeStruct((OWNED * RANK, dl), F32),
            jax.ShapeDtypeStruct((OWNED * RANK, cl), F32),
        ],
        in_specs=[VM],
        out_specs=[VM, VM],
        compiler_params=params(8),
        cost_estimate=cost(0, 2_000_000),
    )(near(bin_parts))
    return (
        key_value_output,
        token_gradient,
        grad_down.reshape(OWNED, RANK, dl),
        grad_up.reshape(OWNED, RANK, cl),
    )


def solution(mesh):
    fine = Mesh(mesh.devices.reshape(NZ, NY, NX, NC), ("z", "y", "x", "c"))
    rows, feat = ("z", "y"), ("x", "c")
    return jax.shard_map(
        on_device,
        mesh=fine,
        in_specs=(
            P(rows, feat),
            P(rows, feat),
            P(feat, rows),
            P(rows, None, feat),
            P(rows, None, feat),
            P(),
            P(),
            P(),
        ),
        out_specs=(
            P(rows, feat),
            P(rows, feat),
            P(rows, None, feat),
            P(rows, None, feat),
        ),
        check_vma=False,
    )
```

```python
import jax
import jax.numpy as jnp
from jax import lax
from jax.experimental import pallas as pl
from jax.experimental.pallas import tpu as pltpu
from jax.sharding import Mesh
from jax.sharding import PartitionSpec as P

NZ, NY, NX, NC = 8, 4, 4, 2
RANK = 32
OWNED = 4
SLOTS = 3
SCALE = 0.5
VM = pl.BlockSpec(memory_space=pltpu.VMEM)
SM = pl.BlockSpec(memory_space=pltpu.SMEM)
ANY = pl.BlockSpec(memory_space=pl.ANY)
HB = pl.BlockSpec(memory_space=pltpu.HBM)
BF = jnp.bfloat16
F32 = jnp.float32


def near(value):
    return pltpu.with_memory_space_constraint(value, pltpu.VMEM)


def far(value):
    return pltpu.with_memory_space_constraint(value, pltpu.HBM)


def made(*shape):
    return pltpu.VMEM(shape, BF)


def made_far(*shape):
    return pltpu.HBM(shape, BF)


def copy_all(pairs, sems):
    copies = [pltpu.make_async_copy(source, target, sems.at[n]) for n, (source, target) in enumerate(pairs)]
    for copy in copies:
        copy.start()
    for copy in copies:
        copy.wait()


def params(mib):
    return pltpu.CompilerParams(vmem_limit_bytes=mib * 1024 * 1024)


def cost(flops, moved):
    return pl.CostEstimate(flops=flops, bytes_accessed=moved, transcendentals=0)


def nt(a, b):
    return lax.dot_general(a, b, (((1,), (1,)), ((), ())), preferred_element_type=F32)


def nn(a, b):
    return lax.dot_general(a, b, (((1,), (0,)), ((), ())), preferred_element_type=F32)


def tn(a, b):
    return lax.dot_general(a, b, (((0,), (0,)), ((), ())), preferred_element_type=F32)


def slot_mask(cut_ref, k, amount):
    row = lax.broadcasted_iota(jnp.int32, (1, amount), 1)
    first, second = cut_ref[0], cut_ref[1]
    if k == 0:
        return row < first
    if k == 1:
        return (row >= first) & (row < second)
    return row >= second


def shift_matrix(yi, amount):
    i = lax.broadcasted_iota(jnp.int32, (amount, amount), 0)
    j = lax.broadcasted_iota(jnp.int32, (amount, amount), 1)
    at = j + yi * (amount // NY)
    at = jnp.where(at >= amount, at - amount, at)
    return (i == at).astype(F32).astype(BF)


def pack_kernel(wt_ref, down_ref, up_ref, out_ref, sems):
    copy_all(
        (
            (wt_ref, out_ref.at[0:64]),
            (down_ref, out_ref.at[64:192]),
            (up_ref.at[0:64], out_ref.at[192:256, 0:256]),
            (up_ref.at[64:128], out_ref.at[192:256, 256:512]),
            (up_ref.at[0:64, 0:128], out_ref.at[192:256, 512:640]),
        ),
        sems,
    )


def turn_kernel(yi_ref, _1, cot_ref, out_ref):
    out_ref[...] = nn(cot_ref[...], shift_matrix(yi_ref[0], cot_ref.shape[1])).astype(BF)


def gather_pieces(all_ref, own, f, b, first):
    for k, piece in enumerate((own, *b, *f[::-1])):
        all_ref[k] = piece[first:]


def pick_kernel(at_ref, own, f1, f2, f3, f4, b1, b2, b3, *refs):
    o0, o1, o2, o3, w_ref, *_, g_ref = refs[NX:]
    gather_pieces(g_ref, own, (f1, f2, f3, f4), (b1, b2, b3), 64)
    for k, piece in enumerate((own, b1, b2, b3, f4, f3, f2, f1)):
        w_ref[k] = piece[:64]
    outs = (o0, o1, o2, o3)
    for k in range(NY):
        for s in range(SLOTS):
            at = at_ref[k * SLOTS + s]
            here = at >= 0
            at = jnp.maximum(at, 0)
            zo, a = at // OWNED, at % OWNED
            down = g_ref[zo, pl.ds(pl.multiple_of(a * RANK, RANK), RANK), :]
            up = g_ref[zo, pl.ds(pl.multiple_of(128 + (a % 2) * RANK, RANK), RANK), :]
            up = jnp.where(a >= 2, up[:, 256:512], up[:, 0:256])
            rows = slice(s * RANK, (s + 1) * RANK)
            outs[k][rows, 0:640] = jnp.where(here, down, jnp.zeros_like(down))
            outs[k][rows, 640:896] = jnp.where(here, up, jnp.zeros_like(up))


def low_kernel(cut_ref, a0, a1, a2, a3, tok_ref, cot_ref, part_ref, slots_ref):
    slots = (a0[...] + a1[...]) + (a2[...] + a3[...])
    slots_ref[...] = slots
    amount = tok_ref.shape[0]
    low = nt(slots[:, :640], tok_ref[...])
    back = nt(slots[:, 640:], cot_ref[...])
    low_sum = jnp.zeros((RANK, amount), F32)
    back_sum = jnp.zeros((RANK, amount), F32)
    for k in range(SLOTS):
        keep = slot_mask(cut_ref, k, amount)
        low_sum += jnp.where(keep, low[k * RANK:(k + 1) * RANK], 0.0)
        back_sum += jnp.where(keep, back[k * RANK:(k + 1) * RANK], 0.0)
    part_ref[0:RANK] = low_sum.astype(BF)
    part_ref[RANK:] = back_sum.astype(BF)


def term_kernel(cut_ref, p0, p1, p2, p3, tok_ref, cot_ref, term_ref, low_ref, back_ref):
    total = (p0[...].astype(F32) + p1[...].astype(F32)) + (p2[...].astype(F32) + p3[...].astype(F32))
    amount = tok_ref.shape[0]
    low, back = total[:RANK], total[RANK:]
    for k in range(SLOTS):
        keep = slot_mask(cut_ref, k, amount)
        low_ref[k * RANK:(k + 1) * RANK] = jnp.where(keep, low, 0.0).astype(BF)
        back_ref[k * RANK:(k + 1) * RANK] = jnp.where(keep, back, 0.0).astype(BF)
    term_ref[:, :640] = (SCALE * nn(back_ref[...], tok_ref[...])).astype(BF)
    term_ref[:, 640:] = (SCALE * nn(low_ref[...], cot_ref[...])).astype(BF)


def pass_kernel(*_):
    pass


def forward_kernel(_1, prev_ref, next_ref, c0, c1, c2, c3, prev_half, next_half, *refs):
    *_, buf_ref, sems = refs
    half = NZ // 2
    copy_all(((prev_ref.at[:half], buf_ref.at[0]), (next_ref.at[half:], buf_ref.at[1])), sems)
    copy_all(((buf_ref.at[0], prev_half), (buf_ref.at[1], next_half)), sems)


def load_weight(refs, w_ref, sems):
    half = NZ // 2
    own, ahead_1, far_low, far_high, behind_1 = refs
    copies = []
    for n, (ref, z, y) in enumerate(
        ((own, slice(0, NZ), 0), (ahead_1, slice(0, NZ), 1), (far_low, slice(0, half), 2), (far_high, slice(half, NZ), 2), (behind_1, slice(0, NZ), 3))
    ):
        copies.append(pltpu.make_async_copy(ref, w_ref.at[z, y * 64:(y + 1) * 64], sems.at[n]))
    for copy in copies:
        copy.start()
    return copies


def load_slices(refs, at_ref, first, w_ref, sems, start):
    half = NZ // 2
    own, ahead_1, far_low, far_high, behind_1 = refs

    def move(ref, z, k, y):
        copy = pltpu.make_async_copy(ref.at[z], w_ref.at[k, y * 64:(y + 1) * 64], sems.at[k, y])
        if start:
            copy.start()
        else:
            copy.wait()

    for k in range(NX):
        at = at_ref[first + k]
        for y, ref in ((0, own), (1, ahead_1), (3, behind_1)):
            move(ref, at, k, y)

        @pl.when(at < half)
        def _(k=k, at=at):
            move(far_low, at, k, 2)

        @pl.when(at >= half)
        def _(k=k, at=at):
            move(far_high, at - half, k, 2)


def wait_all(copies):
    for copy in copies:
        copy.wait()


def kv_send_kernel(at_ref, *refs):
    tok_ref, _, _, out_ref, w_ref, sems = refs[5:]
    load_slices(refs[:5], at_ref, NX, w_ref, sems, True)
    load_slices(refs[:5], at_ref, NX, w_ref, sems, False)

    def step(k, carry):
        out_ref[k] = nt(tok_ref[...], w_ref[k]).astype(BF)
        return carry

    lax.fori_loop(0, NX, step, 0)


def kv_keep_kernel(at_ref, *refs):
    tok_ref, other_ref, *outs, w_ref, sems = refs[5:]
    load_slices(refs[:5], at_ref, 0, w_ref, sems, True)
    load_slices(refs[:5], at_ref, 0, w_ref, sems, False)
    for k, out_ref in enumerate(outs):
        base = nt(tok_ref[...], w_ref[k])
        out_ref[...] = (base + other_ref[k].astype(F32)).astype(BF)


def kv_out_kernel(yi_ref, p0, p1, p2, p3, low_ref, slots_ref, out_ref):
    shift = shift_matrix(yi_ref[0], out_ref.shape[1])
    up = nn(slots_ref[:, 640:], shift).astype(BF)
    total = (p0[...].astype(F32) + p1[...].astype(F32)) + (p2[...].astype(F32) + p3[...].astype(F32))
    total = (total + SCALE * tn(low_ref[...], up)).astype(BF)
    out_ref[...] = nt(total, shift).astype(BF)


def input_grad_kernel(at_ref, *refs):
    cots = refs[5:5 + 2 * NX]
    back_ref, slots_ref, out_ref, acc_ref, w_ref, sems = refs[5 + 2 * NX:]
    copies = load_weight(refs[:5], w_ref, sems)
    acc_ref[...] = SCALE * tn(back_ref[...], slots_ref[:, :640])
    wait_all(copies)
    for k in range(NX):
        acc_ref[...] += nn(cots[k][...], w_ref[at_ref[k]]) + nn(cots[NX + k][...], w_ref[at_ref[NX + k]])
    out_ref[...] = acc_ref[...].astype(BF)


def bin_kernel(to_ref, own, f1, f2, f3, f4, b1, b2, b3, _1, o0, o1, o2, o3, t_ref, acc_ref):
    gather_pieces(t_ref, own, (f1, f2, f3, f4), (b1, b2, b3), 0)
    acc_ref[...] = jnp.zeros_like(acc_ref)
    for j in range(NZ * SLOTS):
        to = to_ref[j]

        @pl.when(to >= 0)
        def _(j=j, to=to):
            zs, s = j // SLOTS, j % SLOTS
            acc_ref[to] += t_ref[zs, s * RANK:(s + 1) * RANK, :].astype(F32)

    for k, o in enumerate((o0, o1, o2, o3)):
        for a in range(OWNED):
            o[a * RANK:(a + 1) * RANK] = acc_ref[k * OWNED + a].astype(BF)


def total_kernel(*refs):
    *parts, down_ref, up_ref = refs
    p0, p1, p2, p3 = (part[...].astype(F32) for part in parts)
    total = (p0 + p1) + (p2 + p3)
    down_ref[...] = total[:, :640]
    up_ref[...] = total[:, 640:]


def others(axis, n, move, values):
    return [values[0]] + [move(values[k], axis, n, k) for k in range(1, n)]


def ahead(value, axis, n, k):
    return lax.ppermute(value, axis, [(i, (i - k) % n) for i in range(n)])


def deliver(value, axis, n, k):
    return lax.ppermute(value, axis, [(i, (i + k) % n) for i in range(n)])


def ring(value):
    f, b = [value], [value]
    for _ in range(NZ // 2 - 1):
        f.append(deliver(f[-1], "z", NZ, 1))
        b.append(deliver(b[-1], "z", NZ, -1))
    f.append(deliver(f[-1], "z", NZ, 1))
    return f[1:] + b[1:]


def on_device(tokens, cot, w, down, up, first_rows, embodiment, store_row):
    zi, yi = lax.axis_index("z"), lax.axis_index("y")
    xi, ci = lax.axis_index("x"), lax.axis_index("c")
    rows, dl = tokens.shape
    cl = cot.shape[1]
    block = zi * NY + yi
    width = dl + cl

    yv = jnp.reshape(yi, (1,)).astype(jnp.int32)
    pack = pl.pallas_call(
        pack_kernel,
        out_shape=made(256, dl),
        in_specs=[HB] * 3,
        out_specs=VM,
        scratch_shapes=[pltpu.SemaphoreType.DMA((5,))],
        compiler_params=params(4),
        cost_estimate=cost(0, 700_000),
    )(far(w.T), far(down.reshape(OWNED * RANK, dl)), far(up.reshape(OWNED * RANK, cl)))
    cot_moved = pl.pallas_call(
        turn_kernel,
        out_shape=made_far(rows, cl),
        in_specs=[SM, ANY, VM],
        out_specs=VM,
        compiler_params=params(4),
        cost_estimate=cost(0, 700_000),
    )(yv, pack, far(cot))
    gathered = ring(pack)
    cot_x = others("x", NX, ahead, [cot_moved] * NX)

    seq_count = first_rows.shape[0]
    emb_hit = embodiment[:, None] == jnp.arange(store_row.shape[0], dtype=jnp.int32)[None, :]
    seq_store = jnp.sum(jnp.where(emb_hit, store_row[None, :], 0), axis=1)

    def stores_of(blocks):
        seqs = (2 * blocks[:, None] - 1 + jnp.arange(SLOTS, dtype=jnp.int32)[None, :]).reshape(-1)
        hit = jnp.maximum(seqs, 0)[:, None] == jnp.arange(seq_count, dtype=jnp.int32)[None, :]
        return jnp.sum(jnp.where(hit, seq_store[None, :], 0), axis=1)

    ks = jnp.arange(NY, dtype=jnp.int32)
    plane = stores_of(zi * NY + (yi + ks) % NY)
    pick_at = jnp.where(
        (plane // OWNED) % NY == yi, ((plane // (OWNED * NY) - zi) % NZ) * OWNED + plane % OWNED, -1
    )
    line = stores_of(((zi + jnp.arange(NZ, dtype=jnp.int32)) % NZ) * NY + yi)
    bin_to = jnp.where(
        line // (OWNED * NY) == zi, (((line // OWNED) % NY - yi) % NY) * OWNED + line % OWNED, -1
    )
    cut = lax.dynamic_slice_in_dim(first_rows, 2 * block, 2) - block * rows
    home = 2 * ((xi + jnp.arange(NX, dtype=jnp.int32)) % NX)
    w_at = jnp.concatenate([home + ci, home + 1 - ci])
    w_at = ((w_at - zi) % NZ).astype(jnp.int32)

    picked = pl.pallas_call(
        pick_kernel,
        out_shape=[made(SLOTS * RANK, width)] * NY
        + [made_far(NZ, 64, dl)]
        + [made_far(rows, cl)] * NX,
        in_specs=[SM] + [VM] * 8 + [ANY] * NX,
        out_specs=[VM] * (NY + 1) + [ANY] * NX,
        input_output_aliases={9 + k: NY + 1 + k for k in range(NX)},
        scratch_shapes=[pltpu.VMEM((NZ, 192, dl), BF)],
        compiler_params=params(6),
        cost_estimate=cost(0, 9_000_000),
    )(pick_at, *map(near, (pack, *gathered)), *map(far, cot_x))
    w_own, cot_x = picked[NY], picked[NY + 1:]
    slot_parts = others("y", NY, deliver, picked)


    part, slots = pl.pallas_call(
        low_kernel,
        out_shape=[
            made(2 * RANK, rows),
            made(SLOTS * RANK, width),
        ],
        in_specs=[SM] + [VM] * 6,
        out_specs=[VM, VM],
        compiler_params=params(6),
        cost_estimate=cost(2 * rows * SLOTS * RANK * width, 3_000_000),
    )(cut, *map(near, slot_parts), tokens, cot)

    w_own = pl.pallas_call(
        pass_kernel,
        out_shape=made_far(NZ, 64, dl),
        in_specs=[VM, ANY],
        out_specs=ANY,
        input_output_aliases={1: 0},
        compiler_params=params(4),
        cost_estimate=cost(0, 1_000),
    )(near(slot_parts[1]), far(w_own))
    w_prev, w_next = deliver(w_own, "y", NY, 1), deliver(w_own, "y", NY, -1)

    part_other = lax.ppermute(part, "c", [(0, 1), (1, 0)])
    part = (part.astype(F32) + part_other.astype(F32)).astype(BF)
    parts = others("x", NX, ahead, [part] * NX)
    term, low, back = pl.pallas_call(
        term_kernel,
        out_shape=[
            made(SLOTS * RANK, width),
            made(SLOTS * RANK, rows),
            made(SLOTS * RANK, rows),
        ],
        in_specs=[SM] + [VM] * 6,
        out_specs=[VM] * 3,
        compiler_params=params(6),
        cost_estimate=cost(2 * rows * SLOTS * RANK * width, 3_000_000),
    )(cut, *map(near, parts), tokens, cot)
    terms = ring(term)
    prev_half, next_half, *cot_x = pl.pallas_call(
        forward_kernel,
        out_shape=[made_far(NZ // 2, 64, dl)] * 2 + [made_far(rows, cl)] * NX,
        in_specs=[ANY, HB, HB] + [ANY] * NX,
        out_specs=[HB, HB] + [ANY] * NX,
        input_output_aliases={3 + k: 2 + k for k in range(NX)},
        scratch_shapes=[pltpu.VMEM((2, NZ // 2, 64, dl), BF), pltpu.SemaphoreType.DMA((2,))],
        compiler_params=params(4),
        cost_estimate=cost(0, 1_000),
    )(term, far(w_prev), far(w_next), *map(far, cot_x))
    far_low, far_high = deliver(prev_half, "y", NY, 1), deliver(next_half, "y", NY, -1)
    ws = [far(v) for v in (w_own, w_next, far_low, far_high, w_prev)]
    cot_other = [lax.ppermute(c, "c", [(0, 1), (1, 0)]) for c in cot_x]

    half = made_far(NX, rows, cl)
    kv_cost = cost(1_000, 1_000)
    kv_send = pl.pallas_call(
        kv_send_kernel,
        out_shape=half,
        in_specs=[SM] + [HB] * 5 + [VM] * 3,
        out_specs=VM,
        scratch_shapes=[pltpu.VMEM((NX, cl, dl), BF), pltpu.SemaphoreType.DMA((NX, NY))],
        compiler_params=params(8),
        cost_estimate=kv_cost,
    )(w_at, *ws, tokens, near(terms[1]), near(terms[NZ // 2 + 1]))
    kv_other = lax.ppermute(kv_send, "c", [(0, 1), (1, 0)])
    kv_keep = pl.pallas_call(
        kv_keep_kernel,
        out_shape=[made_far(rows, cl)] * NX,
        in_specs=[SM] + [HB] * 5 + [VM] * 2,
        out_specs=[VM] * NX,
        scratch_shapes=[pltpu.VMEM((NX, cl, dl), BF), pltpu.SemaphoreType.DMA((NX, NY))],
        compiler_params=params(8),
        cost_estimate=kv_cost,
    )(w_at, *ws, tokens, far(kv_other))
    kv_parts = others("x", NX, deliver, kv_keep)

    token_gradient = pl.pallas_call(
        input_grad_kernel,
        out_shape=jax.ShapeDtypeStruct((rows, dl), BF),
        in_specs=[SM] + [HB] * 5 + [VM] * (2 * NX + 2),
        out_specs=VM,
        scratch_shapes=[
            pltpu.VMEM((rows, dl), F32),
            pltpu.VMEM((NZ, cl, dl), BF),
            pltpu.SemaphoreType.DMA((5,)),
        ],
        compiler_params=params(12),
        cost_estimate=cost(1_000, 1_000),
    )(w_at, *ws, *map(far, (*cot_x, *cot_other)), near(back), near(slots))

    key_value_output = pl.pallas_call(
        kv_out_kernel,
        out_shape=jax.ShapeDtypeStruct((rows, cl), BF),
        in_specs=[SM] + [VM] * 6,
        out_specs=VM,
        compiler_params=params(8),
        cost_estimate=cost(2 * rows * cl * 512, 2_000_000),
    )(yv, *map(far, kv_parts), near(low), near(slots))

    bins = pl.pallas_call(
        bin_kernel,
        out_shape=[made(OWNED * RANK, width)] * NY,
        in_specs=[SM] + [VM] * 8 + [ANY],
        out_specs=[VM] * NY,
        scratch_shapes=[pltpu.VMEM((NZ, SLOTS * RANK, width), BF), pltpu.VMEM((NY * OWNED, RANK, width), F32)],
        compiler_params=params(8),
        cost_estimate=cost(0, 1_000),
    )(bin_to, *map(near, (term, *terms)), far(kv_keep[0]))
    bin_parts = others("y", NY, deliver, bins)
    grad_down, grad_up = pl.pallas_call(
        total_kernel,
        out_shape=[
            jax.ShapeDtypeStruct((OWNED * RANK, dl), F32),
            jax.ShapeDtypeStruct((OWNED * RANK, cl), F32),
        ],
        in_specs=[VM] * NY,
        out_specs=[VM, VM],
        compiler_params=params(8),
        cost_estimate=cost(0, 2_000_000),
    )(*map(near, bin_parts))
    return (
        key_value_output,
        token_gradient,
        grad_down.reshape(OWNED, RANK, dl),
        grad_up.reshape(OWNED, RANK, cl),
    )


def solution(mesh):
    fine = Mesh(mesh.devices.reshape(NZ, NY, NX, NC), ("z", "y", "x", "c"))
    rows, feat = ("z", "y"), ("x", "c")
    return jax.shard_map(
        on_device,
        mesh=fine,
        in_specs=(
            P(rows, feat),
            P(rows, feat),
            P(feat, rows),
            P(rows, None, feat),
            P(rows, None, feat),
            P(),
            P(),
            P(),
        ),
        out_specs=(
            P(rows, feat),
            P(rows, feat),
            P(rows, None, feat),
            P(rows, None, feat),
        ),
        check_vma=False,
    )
```

```python
import jax
import jax.numpy as jnp
from jax import lax
from jax.experimental import pallas as pl
from jax.experimental.pallas import tpu as pltpu
from jax.sharding import Mesh
from jax.sharding import PartitionSpec as P

NZ, NY, NX, NC = 8, 4, 4, 2
RANK = 32
OWNED = 4
SLOTS = 3
SCALE = 0.5
VM = pl.BlockSpec(memory_space=pltpu.VMEM)
SM = pl.BlockSpec(memory_space=pltpu.SMEM)
ANY = pl.BlockSpec(memory_space=pl.ANY)
HB = pl.BlockSpec(memory_space=pltpu.HBM)
BF = jnp.bfloat16
F32 = jnp.float32


def near(value):
    return pltpu.with_memory_space_constraint(value, pltpu.VMEM)


def far(value):
    return pltpu.with_memory_space_constraint(value, pltpu.HBM)


def made(*shape):
    return pltpu.VMEM(shape, BF)


def made_far(*shape):
    return pltpu.HBM(shape, BF)


def copy_all(pairs, sems):
    copies = [pltpu.make_async_copy(source, target, sems.at[n]) for n, (source, target) in enumerate(pairs)]
    for copy in copies:
        copy.start()
    for copy in copies:
        copy.wait()


def params(mib):
    return pltpu.CompilerParams(vmem_limit_bytes=mib * 1024 * 1024)


def cost(flops, moved):
    return pl.CostEstimate(flops=flops, bytes_accessed=moved, transcendentals=0)


def nt(a, b):
    return lax.dot_general(a, b, (((1,), (1,)), ((), ())), preferred_element_type=F32)


def nn(a, b):
    return lax.dot_general(a, b, (((1,), (0,)), ((), ())), preferred_element_type=F32)


def tn(a, b):
    return lax.dot_general(a, b, (((0,), (0,)), ((), ())), preferred_element_type=F32)


def slot_mask(cut_ref, k, amount):
    row = lax.broadcasted_iota(jnp.int32, (1, amount), 1)
    first, second = cut_ref[0], cut_ref[1]
    if k == 0:
        return row < first
    if k == 1:
        return (row >= first) & (row < second)
    return row >= second


def shift_matrix(yi, amount):
    i = lax.broadcasted_iota(jnp.int32, (amount, amount), 0)
    j = lax.broadcasted_iota(jnp.int32, (amount, amount), 1)
    at = j + yi * (amount // NY)
    at = jnp.where(at >= amount, at - amount, at)
    return (i == at).astype(F32).astype(BF)


def pack_kernel(wt_ref, down_ref, up_ref, out_ref, sems):
    copy_all(
        (
            (wt_ref, out_ref.at[0:64]),
            (down_ref, out_ref.at[64:192]),
            (up_ref.at[0:64], out_ref.at[192:256, 0:256]),
            (up_ref.at[64:128], out_ref.at[192:256, 256:512]),
            (up_ref.at[0:64, 0:128], out_ref.at[192:256, 512:640]),
        ),
        sems,
    )


def turn_kernel(yi_ref, _1, cot_ref, out_ref):
    out_ref[...] = nn(cot_ref[...], shift_matrix(yi_ref[0], cot_ref.shape[1])).astype(BF)


def gather_pieces(all_ref, own, f, b, first):
    for k, piece in enumerate((own, *b, *f[::-1])):
        all_ref[k] = piece[first:]


def pick_kernel(at_ref, own, f1, f2, f3, f4, b1, b2, b3, *refs):
    o0, o1, o2, o3, w_ref, *_, g_ref = refs[NX:]
    gather_pieces(g_ref, own, (f1, f2, f3, f4), (b1, b2, b3), 64)
    for k, piece in enumerate((own, b1, b2, b3, f4, f3, f2, f1)):
        w_ref[k] = piece[:64]
    outs = (o0, o1, o2, o3)
    for k in range(NY):
        for s in range(SLOTS):
            at = at_ref[k * SLOTS + s]
            here = at >= 0
            at = jnp.maximum(at, 0)
            zo, a = at // OWNED, at % OWNED
            down = g_ref[zo, pl.ds(pl.multiple_of(a * RANK, RANK), RANK), :]
            up = g_ref[zo, pl.ds(pl.multiple_of(128 + (a % 2) * RANK, RANK), RANK), :]
            up = jnp.where(a >= 2, up[:, 256:512], up[:, 0:256])
            rows = slice(s * RANK, (s + 1) * RANK)
            outs[k][rows, 0:640] = jnp.where(here, down, jnp.zeros_like(down))
            outs[k][rows, 640:896] = jnp.where(here, up, jnp.zeros_like(up))


def low_kernel(cut_ref, a0, a1, a2, a3, tok_ref, cot_ref, part_ref, slots_ref):
    slots = (a0[...] + a1[...]) + (a2[...] + a3[...])
    slots_ref[...] = slots
    amount = tok_ref.shape[0]
    low = nt(slots[:, :640], tok_ref[...])
    back = nt(slots[:, 640:], cot_ref[...])
    low_sum = jnp.zeros((RANK, amount), F32)
    back_sum = jnp.zeros((RANK, amount), F32)
    for k in range(SLOTS):
        keep = slot_mask(cut_ref, k, amount)
        low_sum += jnp.where(keep, low[k * RANK:(k + 1) * RANK], 0.0)
        back_sum += jnp.where(keep, back[k * RANK:(k + 1) * RANK], 0.0)
    part_ref[0:RANK] = low_sum.astype(BF)
    part_ref[RANK:] = back_sum.astype(BF)


def term_kernel(cut_ref, p0, p1, p2, p3, tok_ref, cot_ref, term_ref, low_ref, back_ref):
    total = (p0[...].astype(F32) + p1[...].astype(F32)) + (p2[...].astype(F32) + p3[...].astype(F32))
    amount = tok_ref.shape[0]
    low, back = total[:RANK], total[RANK:]
    for k in range(SLOTS):
        keep = slot_mask(cut_ref, k, amount)
        low_ref[k * RANK:(k + 1) * RANK] = jnp.where(keep, low, 0.0).astype(BF)
        back_ref[k * RANK:(k + 1) * RANK] = jnp.where(keep, back, 0.0).astype(BF)
    term_ref[:, :640] = (SCALE * nn(back_ref[...], tok_ref[...])).astype(BF)
    term_ref[:, 640:] = (SCALE * nn(low_ref[...], cot_ref[...])).astype(BF)


def pass_kernel(*_):
    pass


def forward_kernel(_1, prev_ref, next_ref, c0, c1, c2, c3, prev_half, next_half, *refs):
    *_, buf_ref, sems = refs
    half = NZ // 2
    copy_all(((prev_ref.at[:half], buf_ref.at[0]), (next_ref.at[half:], buf_ref.at[1])), sems)
    copy_all(((buf_ref.at[0], prev_half), (buf_ref.at[1], next_half)), sems)


def load_weight(refs, w_ref, sems):
    half = NZ // 2
    own, ahead_1, far_low, far_high, behind_1 = refs
    copies = []
    for n, (ref, z, y) in enumerate(
        ((own, slice(0, NZ), 0), (ahead_1, slice(0, NZ), 1), (far_low, slice(0, half), 2), (far_high, slice(half, NZ), 2), (behind_1, slice(0, NZ), 3))
    ):
        copies.append(pltpu.make_async_copy(ref, w_ref.at[z, y * 64:(y + 1) * 64], sems.at[n]))
    for copy in copies:
        copy.start()
    return copies


def load_slices(refs, at_ref, first, w_ref, sems, start):
    half = NZ // 2
    own, ahead_1, far_low, far_high, behind_1 = refs

    def move(ref, z, k, y):
        copy = pltpu.make_async_copy(ref.at[z], w_ref.at[k, y * 64:(y + 1) * 64], sems.at[k, y])
        if start:
            copy.start()
        else:
            copy.wait()

    for k in range(NX):
        at = at_ref[first + k]
        for y, ref in ((0, own), (1, ahead_1), (3, behind_1)):
            move(ref, at, k, y)

        @pl.when(at < half)
        def _(k=k, at=at):
            move(far_low, at, k, 2)

        @pl.when(at >= half)
        def _(k=k, at=at):
            move(far_high, at - half, k, 2)


def wait_all(copies):
    for copy in copies:
        copy.wait()


def kv_send_kernel(at_ref, *refs):
    tok_ref, _, _, out_ref, w_ref, sems = refs[5:]
    load_slices(refs[:5], at_ref, NX, w_ref, sems, True)
    load_slices(refs[:5], at_ref, NX, w_ref, sems, False)

    def step(k, carry):
        out_ref[k] = nt(tok_ref[...], w_ref[k]).astype(BF)
        return carry

    lax.fori_loop(0, NX, step, 0)


def kv_keep_kernel(at_ref, *refs):
    tok_ref, other_ref, *outs, w_ref, sems = refs[5:]
    load_slices(refs[:5], at_ref, 0, w_ref, sems, True)
    load_slices(refs[:5], at_ref, 0, w_ref, sems, False)
    for k, out_ref in enumerate(outs):
        base = nt(tok_ref[...], w_ref[k])
        out_ref[...] = (base + other_ref[k].astype(F32)).astype(BF)


def kv_out_kernel(yi_ref, p0, p1, p2, p3, low_ref, slots_ref, out_ref):
    shift = shift_matrix(yi_ref[0], out_ref.shape[1])
    up = nn(slots_ref[:, 640:], shift).astype(BF)
    total = (p0[...].astype(F32) + p1[...].astype(F32)) + (p2[...].astype(F32) + p3[...].astype(F32))
    total = (total + SCALE * tn(low_ref[...], up)).astype(BF)
    out_ref[...] = nt(total, shift).astype(BF)


def input_grad_kernel(at_ref, *refs):
    cots = refs[5:5 + 2 * NX]
    back_ref, slots_ref, out_ref, acc_ref, w_ref, sems = refs[5 + 2 * NX:]
    copies = load_weight(refs[:5], w_ref, sems)
    acc_ref[...] = SCALE * tn(back_ref[...], slots_ref[:, :640])
    wait_all(copies)
    for k in range(NX):
        acc_ref[...] += nn(cots[k][...], w_ref[at_ref[k]]) + nn(cots[NX + k][...], w_ref[at_ref[NX + k]])
    out_ref[...] = acc_ref[...].astype(BF)


def bin_kernel(to_ref, own, f1, f2, f3, f4, b1, b2, b3, _1, o0, o1, o2, o3, t_ref, acc_ref):
    gather_pieces(t_ref, own, (f1, f2, f3, f4), (b1, b2, b3), 0)
    acc_ref[...] = jnp.zeros_like(acc_ref)
    for j in range(NZ * SLOTS):
        to = to_ref[j]

        @pl.when(to >= 0)
        def _(j=j, to=to):
            zs, s = j // SLOTS, j % SLOTS
            acc_ref[to] += t_ref[zs, s * RANK:(s + 1) * RANK, :].astype(F32)

    for k, o in enumerate((o0, o1, o2, o3)):
        for a in range(OWNED):
            o[a * RANK:(a + 1) * RANK] = acc_ref[k * OWNED + a].astype(BF)


def total_kernel(*refs):
    *parts, down_ref, up_ref = refs
    p0, p1, p2, p3 = (part[...].astype(F32) for part in parts)
    total = (p0 + p1) + (p2 + p3)
    down_ref[...] = total[:, :640]
    up_ref[...] = total[:, 640:]


def others(axis, n, move, values):
    return [values[0]] + [move(values[k], axis, n, k) for k in range(1, n)]


def ahead(value, axis, n, k):
    return lax.ppermute(value, axis, [(i, (i - k) % n) for i in range(n)])


def deliver(value, axis, n, k):
    return lax.ppermute(value, axis, [(i, (i + k) % n) for i in range(n)])


def ring(value):
    f, b = [value], [value]
    for _ in range(NZ // 2 - 1):
        f.append(deliver(f[-1], "z", NZ, 1))
        b.append(deliver(b[-1], "z", NZ, -1))
    f.append(deliver(f[-1], "z", NZ, 1))
    return f[1:] + b[1:]


def on_device(tokens, cot, w, down, up, first_rows, embodiment, store_row):
    zi, yi = lax.axis_index("z"), lax.axis_index("y")
    xi, ci = lax.axis_index("x"), lax.axis_index("c")
    rows, dl = tokens.shape
    cl = cot.shape[1]
    block = zi * NY + yi
    width = dl + cl

    yv = jnp.reshape(yi, (1,)).astype(jnp.int32)
    pack = pl.pallas_call(
        pack_kernel,
        out_shape=made(256, dl),
        in_specs=[HB] * 3,
        out_specs=VM,
        scratch_shapes=[pltpu.SemaphoreType.DMA((5,))],
        compiler_params=params(4),
        cost_estimate=cost(0, 700_000),
    )(far(w.T), far(down.reshape(OWNED * RANK, dl)), far(up.reshape(OWNED * RANK, cl)))
    cot_moved = pl.pallas_call(
        turn_kernel,
        out_shape=made_far(rows, cl),
        in_specs=[SM, ANY, VM],
        out_specs=VM,
        compiler_params=params(4),
        cost_estimate=cost(0, 700_000),
    )(yv, pack, far(cot))
    gathered = ring(pack)
    cot_x = others("x", NX, ahead, [cot_moved] * NX)

    seq_count = first_rows.shape[0]
    emb_hit = embodiment[:, None] == jnp.arange(store_row.shape[0], dtype=jnp.int32)[None, :]
    seq_store = jnp.sum(jnp.where(emb_hit, store_row[None, :], 0), axis=1)

    def stores_of(blocks):
        seqs = (2 * blocks[:, None] - 1 + jnp.arange(SLOTS, dtype=jnp.int32)[None, :]).reshape(-1)
        hit = jnp.maximum(seqs, 0)[:, None] == jnp.arange(seq_count, dtype=jnp.int32)[None, :]
        return jnp.sum(jnp.where(hit, seq_store[None, :], 0), axis=1)

    ks = jnp.arange(NY, dtype=jnp.int32)
    plane = stores_of(zi * NY + (yi + ks) % NY)
    pick_at = jnp.where(
        (plane // OWNED) % NY == yi, ((plane // (OWNED * NY) - zi) % NZ) * OWNED + plane % OWNED, -1
    )
    line = stores_of(((zi + jnp.arange(NZ, dtype=jnp.int32)) % NZ) * NY + yi)
    bin_to = jnp.where(
        line // (OWNED * NY) == zi, (((line // OWNED) % NY - yi) % NY) * OWNED + line % OWNED, -1
    )
    cut = lax.dynamic_slice_in_dim(first_rows, 2 * block, 2) - block * rows
    home = 2 * ((xi + jnp.arange(NX, dtype=jnp.int32)) % NX)
    w_at = jnp.concatenate([home + ci, home + 1 - ci])
    w_at = ((w_at - zi) % NZ).astype(jnp.int32)

    picked = pl.pallas_call(
        pick_kernel,
        out_shape=[made(SLOTS * RANK, width)] * NY
        + [made_far(NZ, 64, dl)]
        + [made_far(rows, cl)] * NX,
        in_specs=[SM] + [VM] * 8 + [ANY] * NX,
        out_specs=[VM] * (NY + 1) + [ANY] * NX,
        input_output_aliases={9 + k: NY + 1 + k for k in range(NX)},
        scratch_shapes=[pltpu.VMEM((NZ, 192, dl), BF)],
        compiler_params=params(6),
        cost_estimate=cost(0, 9_000_000),
    )(pick_at, *map(near, (pack, *gathered)), *map(far, cot_x))
    w_own, cot_x = picked[NY], picked[NY + 1:]
    slot_parts = others("y", NY, deliver, picked)


    part, slots = pl.pallas_call(
        low_kernel,
        out_shape=[
            made(2 * RANK, rows),
            made(SLOTS * RANK, width),
        ],
        in_specs=[SM] + [VM] * 6,
        out_specs=[VM, VM],
        compiler_params=params(6),
        cost_estimate=cost(2 * rows * SLOTS * RANK * width, 3_000_000),
    )(cut, *map(near, slot_parts), tokens, cot)

    w_own = pl.pallas_call(
        pass_kernel,
        out_shape=made_far(NZ, 64, dl),
        in_specs=[VM, ANY],
        out_specs=ANY,
        input_output_aliases={1: 0},
        compiler_params=params(4),
        cost_estimate=cost(0, 1_000),
    )(near(slot_parts[1]), far(w_own))
    w_prev, w_next = deliver(w_own, "y", NY, 1), deliver(w_own, "y", NY, -1)

    part_other = lax.ppermute(part, "c", [(0, 1), (1, 0)])
    part = (part.astype(F32) + part_other.astype(F32)).astype(BF)
    parts = others("x", NX, ahead, [part] * NX)
    term, low, back = pl.pallas_call(
        term_kernel,
        out_shape=[
            made(SLOTS * RANK, width),
            made(SLOTS * RANK, rows),
            made(SLOTS * RANK, rows),
        ],
        in_specs=[SM] + [VM] * 6,
        out_specs=[VM] * 3,
        compiler_params=params(6),
        cost_estimate=cost(2 * rows * SLOTS * RANK * width, 3_000_000),
    )(cut, *map(near, parts), tokens, cot)
    terms = ring(term)
    prev_half, next_half, *cot_x = pl.pallas_call(
        forward_kernel,
        out_shape=[made_far(NZ // 2, 64, dl)] * 2 + [made_far(rows, cl)] * NX,
        in_specs=[ANY, HB, HB] + [ANY] * NX,
        out_specs=[HB, HB] + [ANY] * NX,
        input_output_aliases={3 + k: 2 + k for k in range(NX)},
        scratch_shapes=[pltpu.VMEM((2, NZ // 2, 64, dl), BF), pltpu.SemaphoreType.DMA((2,))],
        compiler_params=params(4),
        cost_estimate=cost(0, 1_000),
    )(term, far(w_prev), far(w_next), *map(far, cot_x))
    far_low, far_high = deliver(prev_half, "y", NY, 1), deliver(next_half, "y", NY, -1)
    ws = [far(v) for v in (w_own, w_next, far_low, far_high, w_prev)]
    cot_other = [lax.ppermute(c, "c", [(0, 1), (1, 0)]) for c in cot_x]

    half = made_far(NX, rows, cl)
    kv_cost = cost(1_000, 1_000)
    kv_send = pl.pallas_call(
        kv_send_kernel,
        out_shape=half,
        in_specs=[SM] + [HB] * 5 + [VM] * 3,
        out_specs=VM,
        scratch_shapes=[pltpu.VMEM((NX, cl, dl), BF), pltpu.SemaphoreType.DMA((NX, NY))],
        compiler_params=params(8),
        cost_estimate=kv_cost,
    )(w_at, *ws, tokens, near(terms[1][:16, :128]), near(terms[NZ // 2 + 1][:16, :128]))
    kv_other = lax.ppermute(kv_send, "c", [(0, 1), (1, 0)])
    kv_keep = pl.pallas_call(
        kv_keep_kernel,
        out_shape=[made_far(rows, cl)] * NX,
        in_specs=[SM] + [HB] * 5 + [VM] * 2,
        out_specs=[VM] * NX,
        scratch_shapes=[pltpu.VMEM((NX, cl, dl), BF), pltpu.SemaphoreType.DMA((NX, NY))],
        compiler_params=params(8),
        cost_estimate=kv_cost,
    )(w_at, *ws, tokens, far(kv_other))
    kv_parts = others("x", NX, deliver, kv_keep)

    token_gradient = pl.pallas_call(
        input_grad_kernel,
        out_shape=jax.ShapeDtypeStruct((rows, dl), BF),
        in_specs=[SM] + [HB] * 5 + [VM] * (2 * NX + 2),
        out_specs=VM,
        scratch_shapes=[
            pltpu.VMEM((rows, dl), F32),
            pltpu.VMEM((NZ, cl, dl), BF),
            pltpu.SemaphoreType.DMA((5,)),
        ],
        compiler_params=params(12),
        cost_estimate=cost(1_000, 1_000),
    )(w_at, *ws, *map(far, (*cot_x, *cot_other)), near(back), near(slots))

    key_value_output = pl.pallas_call(
        kv_out_kernel,
        out_shape=jax.ShapeDtypeStruct((rows, cl), BF),
        in_specs=[SM] + [VM] * 6,
        out_specs=VM,
        compiler_params=params(8),
        cost_estimate=cost(2 * rows * cl * 512, 2_000_000),
    )(yv, far(kv_parts[0]), *map(near, kv_parts[1:]), near(low), near(slots))

    bins = pl.pallas_call(
        bin_kernel,
        out_shape=[made(OWNED * RANK, width)] * NY,
        in_specs=[SM] + [VM] * 8 + [ANY],
        out_specs=[VM] * NY,
        scratch_shapes=[pltpu.VMEM((NZ, SLOTS * RANK, width), BF), pltpu.VMEM((NY * OWNED, RANK, width), F32)],
        compiler_params=params(8),
        cost_estimate=cost(0, 1_000),
    )(bin_to, *map(near, (term, *terms)), far(kv_keep[0]))
    bin_parts = others("y", NY, deliver, bins)
    grad_down, grad_up = pl.pallas_call(
        total_kernel,
        out_shape=[
            jax.ShapeDtypeStruct((OWNED * RANK, dl), F32),
            jax.ShapeDtypeStruct((OWNED * RANK, cl), F32),
        ],
        in_specs=[VM] * NY,
        out_specs=[VM, VM],
        compiler_params=params(8),
        cost_estimate=cost(0, 2_000_000),
    )(*map(near, bin_parts))
    return (
        key_value_output,
        token_gradient,
        grad_down.reshape(OWNED, RANK, dl),
        grad_up.reshape(OWNED, RANK, cl),
    )


def solution(mesh):
    fine = Mesh(mesh.devices.reshape(NZ, NY, NX, NC), ("z", "y", "x", "c"))
    rows, feat = ("z", "y"), ("x", "c")
    return jax.shard_map(
        on_device,
        mesh=fine,
        in_specs=(
            P(rows, feat),
            P(rows, feat),
            P(feat, rows),
            P(rows, None, feat),
            P(rows, None, feat),
            P(),
            P(),
            P(),
        ),
        out_specs=(
            P(rows, feat),
            P(rows, feat),
            P(rows, None, feat),
            P(rows, None, feat),
        ),
        check_vma=False,
    )
```

```python
import jax
import jax.numpy as jnp
from jax import lax
from jax.experimental import pallas as pl
from jax.experimental.pallas import tpu as pltpu
from jax.sharding import Mesh
from jax.sharding import PartitionSpec as P

NZ, NY, NX, NC = 8, 4, 4, 2
RANK = 32
OWNED = 4
SLOTS = 3
SCALE = 0.5
VM = pl.BlockSpec(memory_space=pltpu.VMEM)
SM = pl.BlockSpec(memory_space=pltpu.SMEM)
ANY = pl.BlockSpec(memory_space=pl.ANY)
HB = pl.BlockSpec(memory_space=pltpu.HBM)
BF = jnp.bfloat16
F32 = jnp.float32


def near(value):
    return pltpu.with_memory_space_constraint(value, pltpu.VMEM)


def far(value):
    return pltpu.with_memory_space_constraint(value, pltpu.HBM)


def made(*shape):
    return pltpu.VMEM(shape, BF)


def made_far(*shape):
    return pltpu.HBM(shape, BF)


def copy_all(pairs, sems):
    copies = [pltpu.make_async_copy(source, target, sems.at[n]) for n, (source, target) in enumerate(pairs)]
    for copy in copies:
        copy.start()
    for copy in copies:
        copy.wait()


def params(mib):
    return pltpu.CompilerParams(vmem_limit_bytes=mib * 1024 * 1024)


def cost(flops, moved):
    return pl.CostEstimate(flops=flops, bytes_accessed=moved, transcendentals=0)


def nt(a, b):
    return lax.dot_general(a, b, (((1,), (1,)), ((), ())), preferred_element_type=F32)


def nn(a, b):
    return lax.dot_general(a, b, (((1,), (0,)), ((), ())), preferred_element_type=F32)


def tn(a, b):
    return lax.dot_general(a, b, (((0,), (0,)), ((), ())), preferred_element_type=F32)


def slot_mask(cut_ref, k, amount):
    row = lax.broadcasted_iota(jnp.int32, (1, amount), 1)
    first, second = cut_ref[0], cut_ref[1]
    if k == 0:
        return row < first
    if k == 1:
        return (row >= first) & (row < second)
    return row >= second


def shift_matrix(yi, amount):
    i = lax.broadcasted_iota(jnp.int32, (amount, amount), 0)
    j = lax.broadcasted_iota(jnp.int32, (amount, amount), 1)
    at = j + yi * (amount // NY)
    at = jnp.where(at >= amount, at - amount, at)
    return (i == at).astype(F32).astype(BF)


def pack_kernel(wt_ref, down_ref, up_ref, out_ref, sems):
    pairs = []
    for j in range(5):
        columns = slice(j * 128, (j + 1) * 128)
        pairs.append((wt_ref.at[:, columns], out_ref.at[j * 64:(j + 1) * 64]))
        pairs.append((down_ref.at[:, columns], out_ref.at[320 + j * 128:448 + j * 128]))
    for j in range(2):
        pairs.append((up_ref.at[:, j * 128:(j + 1) * 128], out_ref.at[960 + j * 128:1088 + j * 128]))
    copy_all(pairs, sems)


def turn_kernel(yi_ref, _1, cot_ref, out_ref):
    out_ref[...] = nn(cot_ref[...], shift_matrix(yi_ref[0], cot_ref.shape[1])).astype(BF)


def gather_pieces(all_ref, own, f, b, first):
    for k, piece in enumerate((own, *b, *f[::-1])):
        all_ref[k] = piece[first:]


def pick_kernel(at_ref, own, f1, f2, f3, f4, b1, b2, b3, *refs):
    o0, o1, o2, o3, w_ref, *_, g_ref = refs[NX:]
    gather_pieces(g_ref, own, (f1, f2, f3, f4), (b1, b2, b3), 320)
    for k, piece in enumerate((own, b1, b2, b3, f4, f3, f2, f1)):
        for j in range(5):
            w_ref[k, :, j * 128:(j + 1) * 128] = piece[j * 64:(j + 1) * 64]
    outs = (o0, o1, o2, o3)
    for k in range(NY):
        for s in range(SLOTS):
            at = at_ref[k * SLOTS + s]
            here = at >= 0
            at = jnp.maximum(at, 0)
            zo, a = at // OWNED, at % OWNED
            for j in range(7):
                part = g_ref[zo, pl.ds(pl.multiple_of(j * 128 + a * RANK, RANK), RANK), :]
                outs[k][s * RANK:(s + 1) * RANK, j * 128:(j + 1) * 128] = jnp.where(here, part, jnp.zeros_like(part))


def low_kernel(cut_ref, a0, a1, a2, a3, tok_ref, cot_ref, part_ref, slots_ref):
    slots = (a0[...] + a1[...]) + (a2[...] + a3[...])
    slots_ref[...] = slots
    amount = tok_ref.shape[0]
    low = nt(slots[:, :640], tok_ref[...])
    back = nt(slots[:, 640:], cot_ref[...])
    low_sum = jnp.zeros((RANK, amount), F32)
    back_sum = jnp.zeros((RANK, amount), F32)
    for k in range(SLOTS):
        keep = slot_mask(cut_ref, k, amount)
        low_sum += jnp.where(keep, low[k * RANK:(k + 1) * RANK], 0.0)
        back_sum += jnp.where(keep, back[k * RANK:(k + 1) * RANK], 0.0)
    part_ref[0:RANK] = low_sum.astype(BF)
    part_ref[RANK:] = back_sum.astype(BF)


def term_kernel(cut_ref, p0, p1, p2, p3, tok_ref, cot_ref, term_ref, low_ref, back_ref):
    total = (p0[...].astype(F32) + p1[...].astype(F32)) + (p2[...].astype(F32) + p3[...].astype(F32))
    amount = tok_ref.shape[0]
    low, back = total[:RANK], total[RANK:]
    for k in range(SLOTS):
        keep = slot_mask(cut_ref, k, amount)
        low_ref[k * RANK:(k + 1) * RANK] = jnp.where(keep, low, 0.0).astype(BF)
        back_ref[k * RANK:(k + 1) * RANK] = jnp.where(keep, back, 0.0).astype(BF)
    term_ref[:, :640] = (SCALE * nn(back_ref[...], tok_ref[...])).astype(BF)
    term_ref[:, 640:] = (SCALE * nn(low_ref[...], cot_ref[...])).astype(BF)


def pass_kernel(*_):
    pass


def forward_kernel(_1, prev_ref, next_ref, c0, c1, c2, c3, prev_half, next_half, *refs):
    *_, buf_ref, sems = refs
    half = NZ // 2
    copy_all(((prev_ref.at[:half], buf_ref.at[0]), (next_ref.at[half:], buf_ref.at[1])), sems)
    copy_all(((buf_ref.at[0], prev_half), (buf_ref.at[1], next_half)), sems)


def load_weight(refs, w_ref, sems):
    half = NZ // 2
    own, ahead_1, far_low, far_high, behind_1 = refs
    copies = []
    for n, (ref, z, y) in enumerate(
        ((own, slice(0, NZ), 0), (ahead_1, slice(0, NZ), 1), (far_low, slice(0, half), 2), (far_high, slice(half, NZ), 2), (behind_1, slice(0, NZ), 3))
    ):
        copies.append(pltpu.make_async_copy(ref, w_ref.at[z, y * 64:(y + 1) * 64], sems.at[n]))
    for copy in copies:
        copy.start()
    return copies


def load_slices(refs, at_ref, first, w_ref, sems, start):
    half = NZ // 2
    own, ahead_1, far_low, far_high, behind_1 = refs

    def move(ref, z, k, y):
        copy = pltpu.make_async_copy(ref.at[z], w_ref.at[k, y * 64:(y + 1) * 64], sems.at[k, y])
        if start:
            copy.start()
        else:
            copy.wait()

    for k in range(NX):
        at = at_ref[first + k]
        for y, ref in ((0, own), (1, ahead_1), (3, behind_1)):
            move(ref, at, k, y)

        @pl.when(at < half)
        def _(k=k, at=at):
            move(far_low, at, k, 2)

        @pl.when(at >= half)
        def _(k=k, at=at):
            move(far_high, at - half, k, 2)


def wait_all(copies):
    for copy in copies:
        copy.wait()


def kv_send_kernel(at_ref, *refs):
    tok_ref, _, _, out_ref, w_ref, sems = refs[5:]
    load_slices(refs[:5], at_ref, NX, w_ref, sems, True)
    load_slices(refs[:5], at_ref, NX, w_ref, sems, False)

    def step(k, carry):
        out_ref[k] = nt(tok_ref[...], w_ref[k]).astype(BF)
        return carry

    lax.fori_loop(0, NX, step, 0)


def kv_keep_kernel(at_ref, *refs):
    tok_ref, other_ref, *outs, w_ref, sems = refs[5:]
    load_slices(refs[:5], at_ref, 0, w_ref, sems, True)
    load_slices(refs[:5], at_ref, 0, w_ref, sems, False)
    for k, out_ref in enumerate(outs):
        base = nt(tok_ref[...], w_ref[k])
        out_ref[...] = (base + other_ref[k].astype(F32)).astype(BF)


def kv_out_kernel(yi_ref, p0, p1, p2, p3, low_ref, slots_ref, out_ref):
    shift = shift_matrix(yi_ref[0], out_ref.shape[1])
    up = nn(slots_ref[:, 640:], shift).astype(BF)
    total = (p0[...].astype(F32) + p1[...].astype(F32)) + (p2[...].astype(F32) + p3[...].astype(F32))
    total = (total + SCALE * tn(low_ref[...], up)).astype(BF)
    out_ref[...] = nt(total, shift).astype(BF)


def input_grad_kernel(at_ref, *refs):
    cots = refs[5:5 + 2 * NX]
    back_ref, slots_ref, out_ref, acc_ref, w_ref, sems = refs[5 + 2 * NX:]
    copies = load_weight(refs[:5], w_ref, sems)
    acc_ref[...] = SCALE * tn(back_ref[...], slots_ref[:, :640])
    wait_all(copies)
    for k in range(NX):
        acc_ref[...] += nn(cots[k][...], w_ref[at_ref[k]]) + nn(cots[NX + k][...], w_ref[at_ref[NX + k]])
    out_ref[...] = acc_ref[...].astype(BF)


def bin_kernel(to_ref, own, f1, f2, f3, f4, b1, b2, b3, _1, o0, o1, o2, o3, t_ref, acc_ref):
    gather_pieces(t_ref, own, (f1, f2, f3, f4), (b1, b2, b3), 0)
    acc_ref[...] = jnp.zeros_like(acc_ref)
    for j in range(NZ * SLOTS):
        to = to_ref[j]

        @pl.when(to >= 0)
        def _(j=j, to=to):
            zs, s = j // SLOTS, j % SLOTS
            acc_ref[to] += t_ref[zs, s * RANK:(s + 1) * RANK, :].astype(F32)

    for k, o in enumerate((o0, o1, o2, o3)):
        for a in range(OWNED):
            o[a * RANK:(a + 1) * RANK] = acc_ref[k * OWNED + a].astype(BF)


def total_kernel(*refs):
    *parts, down_ref, up_ref = refs
    p0, p1, p2, p3 = (part[...].astype(F32) for part in parts)
    total = (p0 + p1) + (p2 + p3)
    down_ref[...] = total[:, :640]
    up_ref[...] = total[:, 640:]


def others(axis, n, move, values):
    return [values[0]] + [move(values[k], axis, n, k) for k in range(1, n)]


def ahead(value, axis, n, k):
    return lax.ppermute(value, axis, [(i, (i - k) % n) for i in range(n)])


def deliver(value, axis, n, k):
    return lax.ppermute(value, axis, [(i, (i + k) % n) for i in range(n)])


def ring(value):
    f, b = [value], [value]
    for _ in range(NZ // 2 - 1):
        f.append(deliver(f[-1], "z", NZ, 1))
        b.append(deliver(b[-1], "z", NZ, -1))
    f.append(deliver(f[-1], "z", NZ, 1))
    return f[1:] + b[1:]


def on_device(tokens, cot, w, down, up, first_rows, embodiment, store_row):
    zi, yi = lax.axis_index("z"), lax.axis_index("y")
    xi, ci = lax.axis_index("x"), lax.axis_index("c")
    rows, dl = tokens.shape
    cl = cot.shape[1]
    block = zi * NY + yi
    width = dl + cl

    yv = jnp.reshape(yi, (1,)).astype(jnp.int32)
    pack = pl.pallas_call(
        pack_kernel,
        out_shape=made(1216, 128),
        in_specs=[HB] * 3,
        out_specs=VM,
        scratch_shapes=[pltpu.SemaphoreType.DMA((12,))],
        compiler_params=params(4),
        cost_estimate=cost(0, 700_000),
    )(far(w.T), far(down.reshape(OWNED * RANK, dl)), far(up.reshape(OWNED * RANK, cl)))
    cot_moved = pl.pallas_call(
        turn_kernel,
        out_shape=made_far(rows, cl),
        in_specs=[SM, ANY, VM],
        out_specs=VM,
        compiler_params=params(4),
        cost_estimate=cost(0, 700_000),
    )(yv, pack, far(cot))
    gathered = ring(pack)
    cot_x = others("x", NX, ahead, [cot_moved] * NX)

    seq_count = first_rows.shape[0]
    emb_hit = embodiment[:, None] == jnp.arange(store_row.shape[0], dtype=jnp.int32)[None, :]
    seq_store = jnp.sum(jnp.where(emb_hit, store_row[None, :], 0), axis=1)

    def stores_of(blocks):
        seqs = (2 * blocks[:, None] - 1 + jnp.arange(SLOTS, dtype=jnp.int32)[None, :]).reshape(-1)
        hit = jnp.maximum(seqs, 0)[:, None] == jnp.arange(seq_count, dtype=jnp.int32)[None, :]
        return jnp.sum(jnp.where(hit, seq_store[None, :], 0), axis=1)

    ks = jnp.arange(NY, dtype=jnp.int32)
    plane = stores_of(zi * NY + (yi + ks) % NY)
    pick_at = jnp.where(
        (plane // OWNED) % NY == yi, ((plane // (OWNED * NY) - zi) % NZ) * OWNED + plane % OWNED, -1
    )
    line = stores_of(((zi + jnp.arange(NZ, dtype=jnp.int32)) % NZ) * NY + yi)
    bin_to = jnp.where(
        line // (OWNED * NY) == zi, (((line // OWNED) % NY - yi) % NY) * OWNED + line % OWNED, -1
    )
    cut = lax.dynamic_slice_in_dim(first_rows, 2 * block, 2) - block * rows
    home = 2 * ((xi + jnp.arange(NX, dtype=jnp.int32)) % NX)
    w_at = jnp.concatenate([home + ci, home + 1 - ci])
    w_at = ((w_at - zi) % NZ).astype(jnp.int32)

    picked = pl.pallas_call(
        pick_kernel,
        out_shape=[made(SLOTS * RANK, width)] * NY
        + [made_far(NZ, 64, dl)]
        + [made_far(rows, cl)] * NX,
        in_specs=[SM] + [VM] * 8 + [ANY] * NX,
        out_specs=[VM] * (NY + 1) + [ANY] * NX,
        input_output_aliases={9 + k: NY + 1 + k for k in range(NX)},
        scratch_shapes=[pltpu.VMEM((NZ, 896, 128), BF)],
        compiler_params=params(6),
        cost_estimate=cost(0, 9_000_000),
    )(pick_at, *map(near, (pack, *gathered)), *map(far, cot_x))
    w_own, cot_x = picked[NY], picked[NY + 1:]
    slot_parts = others("y", NY, deliver, picked)


    part, slots = pl.pallas_call(
        low_kernel,
        out_shape=[
            made(2 * RANK, rows),
            made(SLOTS * RANK, width),
        ],
        in_specs=[SM] + [VM] * 6,
        out_specs=[VM, VM],
        compiler_params=params(6),
        cost_estimate=cost(2 * rows * SLOTS * RANK * width, 3_000_000),
    )(cut, *map(near, slot_parts), tokens, cot)

    w_own = pl.pallas_call(
        pass_kernel,
        out_shape=made_far(NZ, 64, dl),
        in_specs=[VM, ANY],
        out_specs=ANY,
        input_output_aliases={1: 0},
        compiler_params=params(4),
        cost_estimate=cost(0, 1_000),
    )(near(slot_parts[1]), far(w_own))
    w_prev, w_next = deliver(w_own, "y", NY, 1), deliver(w_own, "y", NY, -1)

    part_other = lax.ppermute(part, "c", [(0, 1), (1, 0)])
    part = (part.astype(F32) + part_other.astype(F32)).astype(BF)
    parts = others("x", NX, ahead, [part] * NX)
    term, low, back = pl.pallas_call(
        term_kernel,
        out_shape=[
            made(SLOTS * RANK, width),
            made(SLOTS * RANK, rows),
            made(SLOTS * RANK, rows),
        ],
        in_specs=[SM] + [VM] * 6,
        out_specs=[VM] * 3,
        compiler_params=params(6),
        cost_estimate=cost(2 * rows * SLOTS * RANK * width, 3_000_000),
    )(cut, *map(near, parts), tokens, cot)
    terms = ring(term)
    prev_half, next_half, *cot_x = pl.pallas_call(
        forward_kernel,
        out_shape=[made_far(NZ // 2, 64, dl)] * 2 + [made_far(rows, cl)] * NX,
        in_specs=[ANY, HB, HB] + [ANY] * NX,
        out_specs=[HB, HB] + [ANY] * NX,
        input_output_aliases={3 + k: 2 + k for k in range(NX)},
        scratch_shapes=[pltpu.VMEM((2, NZ // 2, 64, dl), BF), pltpu.SemaphoreType.DMA((2,))],
        compiler_params=params(4),
        cost_estimate=cost(0, 1_000),
    )(term, far(w_prev), far(w_next), *map(far, cot_x))
    far_low, far_high = deliver(prev_half, "y", NY, 1), deliver(next_half, "y", NY, -1)
    ws = [far(v) for v in (w_own, w_next, far_low, far_high, w_prev)]
    cot_other = [lax.ppermute(c, "c", [(0, 1), (1, 0)]) for c in cot_x]

    half = made_far(NX, rows, cl)
    kv_cost = cost(1_000, 1_000)
    kv_send = pl.pallas_call(
        kv_send_kernel,
        out_shape=half,
        in_specs=[SM] + [HB] * 5 + [VM] * 3,
        out_specs=VM,
        scratch_shapes=[pltpu.VMEM((NX, cl, dl), BF), pltpu.SemaphoreType.DMA((NX, NY))],
        compiler_params=params(8),
        cost_estimate=kv_cost,
    )(w_at, *ws, tokens, near(terms[1][:16, :128]), near(terms[NZ // 2 + 1][:16, :128]))
    kv_other = lax.ppermute(kv_send, "c", [(0, 1), (1, 0)])
    kv_keep = pl.pallas_call(
        kv_keep_kernel,
        out_shape=[made_far(rows, cl)] * NX,
        in_specs=[SM] + [HB] * 5 + [VM] * 2,
        out_specs=[VM] * NX,
        scratch_shapes=[pltpu.VMEM((NX, cl, dl), BF), pltpu.SemaphoreType.DMA((NX, NY))],
        compiler_params=params(8),
        cost_estimate=kv_cost,
    )(w_at, *ws, tokens, far(kv_other))
    kv_parts = others("x", NX, deliver, kv_keep)

    token_gradient = pl.pallas_call(
        input_grad_kernel,
        out_shape=jax.ShapeDtypeStruct((rows, dl), BF),
        in_specs=[SM] + [HB] * 5 + [VM] * (2 * NX + 2),
        out_specs=VM,
        scratch_shapes=[
            pltpu.VMEM((rows, dl), F32),
            pltpu.VMEM((NZ, cl, dl), BF),
            pltpu.SemaphoreType.DMA((5,)),
        ],
        compiler_params=params(12),
        cost_estimate=cost(1_000, 1_000),
    )(w_at, *ws, *map(far, (*cot_x, *cot_other)), near(back), near(slots))

    key_value_output = pl.pallas_call(
        kv_out_kernel,
        out_shape=jax.ShapeDtypeStruct((rows, cl), BF),
        in_specs=[SM] + [VM] * 6,
        out_specs=VM,
        compiler_params=params(8),
        cost_estimate=cost(2 * rows * cl * 512, 2_000_000),
    )(yv, far(kv_parts[0]), *map(near, kv_parts[1:]), near(low), near(slots))

    bins = pl.pallas_call(
        bin_kernel,
        out_shape=[made(OWNED * RANK, width)] * NY,
        in_specs=[SM] + [VM] * 8 + [ANY],
        out_specs=[VM] * NY,
        scratch_shapes=[pltpu.VMEM((NZ, SLOTS * RANK, width), BF), pltpu.VMEM((NY * OWNED, RANK, width), F32)],
        compiler_params=params(8),
        cost_estimate=cost(0, 1_000),
    )(bin_to, *map(near, (term, *terms)), far(kv_keep[0]))
    bin_parts = others("y", NY, deliver, bins)
    grad_down, grad_up = pl.pallas_call(
        total_kernel,
        out_shape=[
            jax.ShapeDtypeStruct((OWNED * RANK, dl), F32),
            jax.ShapeDtypeStruct((OWNED * RANK, cl), F32),
        ],
        in_specs=[VM] * NY,
        out_specs=[VM, VM],
        compiler_params=params(8),
        cost_estimate=cost(0, 2_000_000),
    )(*map(near, bin_parts))
    return (
        key_value_output,
        token_gradient,
        grad_down.reshape(OWNED, RANK, dl),
        grad_up.reshape(OWNED, RANK, cl),
    )


def solution(mesh):
    fine = Mesh(mesh.devices.reshape(NZ, NY, NX, NC), ("z", "y", "x", "c"))
    rows, feat = ("z", "y"), ("x", "c")
    return jax.shard_map(
        on_device,
        mesh=fine,
        in_specs=(
            P(rows, feat),
            P(rows, feat),
            P(feat, rows),
            P(rows, None, feat),
            P(rows, None, feat),
            P(),
            P(),
            P(),
        ),
        out_specs=(
            P(rows, feat),
            P(rows, feat),
            P(rows, None, feat),
            P(rows, None, feat),
        ),
        check_vma=False,
    )
```
